32 devices in a mesh: lvl: 2 (over x), row: 16 (over z, y, core).
Axes of the slice: x: 2, y: 2, z: 4, core: 2. Of those that a mesh axis runs over, the one named last changes fastest.
Arguments:
- rhs: float32 [2, 16, 3, 128, 128], P('lvl', 'row'), may hold values from -6 to 6
- op_tiles: float32 [2, 16, 3, 7, 128, 128], P('lvl', 'row'), may hold values from -1 to 4
- op_cols: int32 [2, 16, 3, 7], P('lvl', 'row'), may hold values from 0 to 8, as said below
- link_tiles: float32 [2, 16, 3, 2, 128, 128], P('lvl', 'row'), may hold values from -0.3125 to 0.3125
- level_links: int32 [2, 16, 3, 2], P('lvl', 'row'), may hold values from 0 to 1, as said below
Outputs:
- levels: float32 [2, 16, 3, 128, 128], P('lvl', 'row')
The draws below stay inside these ranges and needn't reach their ends.
Inputs may be any that keep to these rules, and one draw needn't show every extreme that they name: `op_cols`: tile 0 of each block row has code 3 + s (the block itself). Fine blocks have 7 distinct codes; every other block names only codes s, 3 + s, 6 + s of its own slot s. `level_links`: entries of blocks that are not fine are 0.
All inputs are finite; a program needn't handle non-finite values.
Results may differ from the reference program's by a relative error of at most 0.00021.
Values sent between devices are 32-bit elements; how exact they have to be, the bound alone decides.
No kernel may reach another device: no remote copies, remote signals or barrier semaphores. Data moves between devices by JAX's collectives and lax.ppermute only.
A program may use at most 64 MiB of HBM per device.

```python
import math
import jax
import jax.numpy as jnp
from jax import lax

BLK = 128
NRHS = 128
SLOTS = 3
OPT = 7
CYCLES = 2
LFINE = 1
LMID = 1
N_LVL = 2
N_ROW = 16


def draw_op_tiles(key, part):
    shape = (N_LVL, N_ROW, SLOTS, OPT, BLK, BLK)
    noise = jax.random.normal(key, shape, jnp.float32)
    first = jnp.where(jnp.arange(OPT) == 0, 1.0, 0.0).astype(jnp.float32)
    eye = jnp.eye(BLK, dtype=jnp.float32)
    return noise * (0.2 / math.sqrt(BLK)) + 2.5 * first[:, None, None] * eye


def draw_op_cols(key, part):
    lvl_ids = jnp.arange(N_LVL)[:, None, None, None]
    slot_ids = jnp.arange(SLOTS)[None, None, :, None]
    count = N_LVL * N_ROW * SLOTS
    keys = jax.random.split(jax.random.fold_in(key, 11), count)
    orders = jax.vmap(lambda one: jax.random.permutation(one, 3 * SLOTS - 1))(keys)
    orders = orders.reshape((N_LVL, N_ROW, SLOTS, 3 * SLOTS - 1))[..., :OPT - 1]
    own = SLOTS + slot_ids
    fine_rest = (own + 1 + orders) % (3 * SLOTS)
    steps = jax.random.randint(jax.random.fold_in(key, 12), (N_LVL, N_ROW, SLOTS, OPT - 1), 0, 3)
    drawn_rest = steps * SLOTS + slot_ids
    rest = jnp.where(lvl_ids < LFINE, fine_rest, drawn_rest)
    own_full = jnp.broadcast_to(own, (N_LVL, N_ROW, SLOTS, 1))
    return jnp.concatenate([own_full, rest], axis=3).astype(jnp.int32)


def draw_level_links(key, part):
    lvl_ids = jnp.arange(N_LVL)[:, None, None, None]
    picks = jax.random.randint(jax.random.fold_in(key, 21), (N_LVL, N_ROW, SLOTS, 2), 0, 2 * LMID)
    return jnp.where(lvl_ids < LFINE, picks, 0).astype(jnp.int32)


def block_scale(own_key, shape, shards, low, high):
    factor_of, own = 1.0, jax.random.fold_in(own_key, 6)
    for position, parts in shards:
        draws = jnp.exp(jax.random.uniform(jax.random.fold_in(own, position), (parts,), jnp.float32, low / len(shards), high / len(shards)))
        factor_of = factor_of * jnp.repeat(draws, shape[position] // parts).reshape([-1 if axis == position else 1 for axis in range(len(shape))])
    return factor_of


def gaussian(rng, shape, deviation, bound, cuts=(), kind=jnp.bfloat16):
    drawn = jax.random.normal(rng, shape, jnp.float32) * deviation
    if len(cuts) > 0:
        drawn = block_scale(rng, shape, cuts, -0.22, 0.18) * drawn
    return jnp.clip(drawn, min=-bound, max=bound).astype(kind)


def setup_inputs(seed: int = 0) -> dict:
    seeds = jax.random.split(jax.random.key(seed), 6)
    return {
        "rhs": gaussian(seeds[0], (N_LVL, N_ROW, SLOTS, BLK, NRHS), 1.0, 6.0, ((0, 2), (1, 16)), jnp.float32),
        "op_tiles": draw_op_tiles(jax.random.fold_in(seeds[5], 71), 0),
        "op_cols": draw_op_cols(jax.random.fold_in(seeds[5], 71), 0),
        "link_tiles": gaussian(seeds[3], (N_LVL, N_ROW, SLOTS, 2, BLK, BLK), (BLK * SLOTS) ** -0.5, 0.3125, ((0, 2), (1, 16)), jnp.float32),
        "level_links": draw_level_links(jax.random.fold_in(seeds[5], 71), 0),
    }


HIGH = lax.Precision.HIGHEST
COEF_ZERO = 0.9
COEF_ONE = -0.36
COEF_TWO = 0.05


def level_masks():
    lvl_ids = jnp.arange(N_LVL)[:, None]
    slot_ids = jnp.arange(SLOTS)[None, :]
    fine = jnp.where((lvl_ids < LFINE) & (slot_ids >= 0), 1.0, 0.0).astype(jnp.float32)
    mid_slot = (slot_ids == 0) | (slot_ids == 2)
    mid = jnp.where((lvl_ids >= LFINE) & (lvl_ids < LFINE + LMID) & mid_slot, 1.0, 0.0).astype(jnp.float32)
    coarse = jnp.where((lvl_ids == N_LVL - 1) & (slot_ids == 1), 1.0, 0.0).astype(jnp.float32)
    return fine, mid, coarse


def spread(mask):
    return mask[:, None, :, None, None]


def take_mid(field):
    sub = field[LFINE:LFINE + LMID][:, :, 0:3:2]
    sub = jnp.moveaxis(sub, 2, 1)
    return sub.reshape((2 * LMID,) + sub.shape[2:])


def put_mid(field, values):
    values = values.reshape((LMID, 2) + values.shape[1:])
    values = jnp.moveaxis(values, 1, 2)
    field = field.at[LFINE:LFINE + LMID, :, 0].set(values[:, :, 0])
    return field.at[LFINE:LFINE + LMID, :, 2].set(values[:, :, 1])


def apply_operator(field, op_tiles, op_cols, keep):
    edge = jnp.zeros_like(field[:, :1])
    padded = jnp.concatenate([edge, field, edge], axis=1)

    def one_level(items):
        pad_level, tiles_level, cols_level = items
        candidates = jnp.stack([pad_level[:-2], pad_level[1:-1], pad_level[2:]], axis=1)
        candidates = candidates.reshape((N_ROW, 3 * SLOTS, BLK, NRHS))
        picked = jax.vmap(lambda cand, cols: cand[cols])(candidates, cols_level)
        return jnp.einsum("rsjab,rsjbn->rsan", tiles_level, picked, precision=HIGH)

    image = lax.map(one_level, (padded, op_tiles, op_cols))
    return image * spread(keep)


def reference(rhs, op_tiles, op_cols, link_tiles, level_links):
    fine, mid, coarse = level_masks()
    keep = fine + mid + coarse
    mid_ids = jnp.arange(2 * LMID)
    to_mid = (level_links[..., 0][..., None] == mid_ids).astype(jnp.float32) * fine[:, None, :, None]
    from_mid = (level_links[..., 1][..., None] == mid_ids).astype(jnp.float32) * fine[:, None, :, None]
    restrict = link_tiles[:, :, :, 0]
    prolong = link_tiles[:, :, :, 1]
    mid_restrict = take_mid(restrict)
    mid_prolong = take_mid(prolong)
    solution = jnp.zeros_like(rhs)
    mid_fix = jnp.zeros((2 * LMID, N_ROW, BLK, NRHS), jnp.float32)
    coarse_fix = jnp.zeros((N_ROW, BLK, NRHS), jnp.float32)
    for cycle in range(CYCLES):
        if cycle == 0:
            resid = rhs * spread(fine)
        else:
            resid = (rhs - apply_operator(solution, op_tiles, op_cols, keep)) * spread(fine)
        terms = jnp.einsum("lrsab,lrsbn->lrsan", restrict, resid, precision=HIGH)
        mid_resid = jnp.einsum("lrsk,lrsan->kran", to_mid, terms, precision=HIGH)
        fine_sum = jnp.sum(terms * spread(fine), axis=(0, 2))
        coarse_resid = jnp.einsum("krab,krbn->ran", mid_restrict, mid_resid, precision=HIGH) + 0.5 * fine_sum
        level_resid = put_mid(resid, mid_resid)
        level_resid = level_resid.at[N_LVL - 1, :, 1].set(coarse_resid)
        first = apply_operator(level_resid, op_tiles, op_cols, keep)
        second = apply_operator(first, op_tiles, op_cols, keep)
        smooth = COEF_ZERO * level_resid + COEF_ONE * first + COEF_TWO * second
        coarse_fix = smooth[N_LVL - 1, :, 1]
        mid_fix = take_mid(smooth) + jnp.einsum("krab,rbn->kran", mid_prolong, coarse_fix, precision=HIGH)
        chosen = jnp.einsum("lrsk,kran->lrsan", from_mid, mid_fix, precision=HIGH)
        chosen = chosen + coarse_fix[None, :, None]
        fine_fix = smooth + jnp.einsum("lrsab,lrsbn->lrsan", prolong, chosen, precision=HIGH)
        solution = solution + fine_fix * spread(fine)
    levels = put_mid(solution, mid_fix)
    levels = levels.at[N_LVL - 1, :, 1].set(coarse_fix)
    return levels
```

```python
import functools

import jax
import jax.numpy as jnp
from jax import lax
from jax.experimental import pallas as pl
from jax.experimental.pallas import tpu as pltpu
from jax.sharding import PartitionSpec as P

CYCLES = 2


HIGH = lax.Precision.HIGHEST
COEF_ZERO = 0.9
COEF_ONE = -0.36
COEF_TWO = 0.05
F32 = jnp.float32
BF16 = jnp.bfloat16


def extended(block, sides, width):
    for axis, dim in sides:
        count = lax.axis_size(axis)
        forward = [(i, i + 1) for i in range(count - 1)]
        backward = [(target, source) for source, target in forward]
        low = lax.ppermute(
            lax.slice_in_dim(block, block.shape[dim] - width, None, axis=dim), axis, forward
        )
        high = lax.ppermute(lax.slice_in_dim(block, 0, width, axis=dim), axis, backward)
        block = jnp.concatenate([low, block, high], axis=dim)
    return block


def broadcast(block, axis, source):
    block = jnp.where(lax.axis_index(axis) == source, block, jnp.zeros_like(block))
    return lax.psum(block, axis)


def apply_operator(field, tiles, columns, keep):
    slots = field.shape[0]
    padded = extended(field[None], (("row", 0),), 1)
    candidates = padded.reshape((3 * slots,) + field.shape[1:])
    picked = candidates[columns]
    image = jnp.einsum("sjab,sjbn->san", tiles, picked, precision=HIGH)
    return image * keep[:, None, None]


def per_device(rhs, op_tiles, op_cols, link_tiles, level_links):
    n_lvl = lax.axis_size("lvl")
    fine_lvls = 5 * n_lvl // 8
    mid_lvls = max(n_lvl - fine_lvls - 1, 1)
    lvl_here = lax.axis_index("lvl")
    right = rhs[0, 0]
    tiles = op_tiles[0, 0]
    columns = op_cols[0, 0]
    links = link_tiles[0, 0]
    targets = level_links[0, 0]
    slots = right.shape[0]
    slot_ids = jnp.arange(slots)
    pair_ids = jnp.arange(2)
    is_fine = lvl_here < fine_lvls
    is_mid = (lvl_here >= fine_lvls) & (lvl_here < fine_lvls + mid_lvls)
    is_coarse = lvl_here == n_lvl - 1
    fine_keep = jnp.where(is_fine & (slot_ids >= 0), 1.0, 0.0).astype(jnp.float32)
    mid_keep = jnp.where(is_mid & ((slot_ids == 0) | (slot_ids == 2)), 1.0, 0.0).astype(jnp.float32)
    coarse_keep = jnp.where(is_coarse & (slot_ids == 1), 1.0, 0.0).astype(jnp.float32)
    all_keep = fine_keep + mid_keep + coarse_keep
    mid_flag = jnp.where(is_mid, 1.0, 0.0).astype(jnp.float32)
    place = (slot_ids[:, None] == 2 * pair_ids[None, :]).astype(jnp.float32) * mid_flag
    lvl_ids = jnp.arange(n_lvl)

    def lvl_table(target):
        by_lvl = (target[:, None] // 2 + fine_lvls == lvl_ids[None, :]).astype(jnp.float32)
        by_pair = (target[:, None] % 2 == pair_ids[None, :]).astype(jnp.float32)
        return by_lvl[:, :, None] * by_pair[:, None, :] * fine_keep[:, None, None]

    to_lvl = lvl_table(targets[:, 0])
    from_lvl = lvl_table(targets[:, 1])
    mid_restrict = jnp.stack([links[0, 0], links[2, 0]])
    mid_prolong = jnp.stack([links[0, 1], links[2, 1]])
    solution = jnp.zeros_like(right)
    mid_fix = jnp.zeros((2,) + right.shape[1:], jnp.float32)
    coarse_fix = jnp.zeros_like(right[0])
    for cycle in range(CYCLES):
        if cycle == 0:
            resid = right * fine_keep[:, None, None]
        else:
            resid = (right - apply_operator(solution, tiles, columns, all_keep)) * fine_keep[
                :, None, None
            ]
        terms = jnp.einsum("sab,sbn->san", links[:, 0], resid, precision=HIGH)
        dense = jnp.einsum("slm,san->lman", to_lvl, terms, precision=HIGH)
        mid_resid = lax.psum_scatter(dense, "lvl", scatter_dimension=0, tiled=True)[0] * mid_flag
        mid_part = jnp.einsum("mab,mbn->an", mid_restrict, mid_resid, precision=HIGH) * mid_flag
        fine_part = 0.5 * jnp.sum(terms * fine_keep[:, None, None], axis=0)
        coarse_resid = lax.psum(mid_part + fine_part, "lvl")
        level_resid = resid + jnp.einsum("sm,man->san", place, mid_resid, precision=HIGH)
        level_resid = level_resid + coarse_keep[:, None, None] * coarse_resid[None]
        first = apply_operator(level_resid, tiles, columns, all_keep)
        second = apply_operator(first, tiles, columns, all_keep)
        smooth = COEF_ZERO * level_resid + COEF_ONE * first + COEF_TWO * second
        coarse_fix = broadcast(smooth[1], "lvl", n_lvl - 1)
        mid_fix = jnp.stack([smooth[0], smooth[2]]) + jnp.einsum(
            "mab,bn->man", mid_prolong, coarse_fix, precision=HIGH
        )
        gathered = lax.all_gather(mid_fix[None], "lvl", axis=0, tiled=True)
        chosen = jnp.einsum("slm,lman->san", from_lvl, gathered, precision=HIGH)
        chosen = chosen + coarse_fix[None]
        fine_fix = smooth + jnp.einsum("sab,sbn->san", links[:, 1], chosen, precision=HIGH)
        solution = solution + fine_fix * fine_keep[:, None, None]
    levels = solution * fine_keep[:, None, None] + jnp.einsum(
        "sm,man->san", place, mid_fix, precision=HIGH
    )
    levels = levels + coarse_keep[:, None, None] * coarse_fix[None]
    return levels[None, None]


def split(value):
    high = value.astype(BF16)
    return high, (value - high.astype(F32)).astype(BF16)


def split_rows(value):
    return jnp.concatenate(split(value), axis=0)


def split_columns(value):
    return jnp.concatenate(split(value), axis=1)


def product(left, right):
    full = jnp.dot(left, right, preferred_element_type=F32)
    rows, columns = full.shape[0] // 2, full.shape[1] // 2
    small = full[rows:, :columns] + full[:rows, columns:] + full[rows:, columns:]
    return full[:rows, :columns] + small


def stacked(*blocks):
    return jnp.concatenate(blocks, axis=0)


def restrict_kernel(targets, rhs, links, mids, payload, restrict, prolong):
    size = rhs.shape[-1]
    slots = rhs.shape[0]

    @pl.when(lax.axis_index("lvl") == 0)
    def _():
        payload[...] = rhs[...]
        for s in range(slots):
            for k in range(2):
                down = jnp.where(targets[s, 0] == k, links[s, 0], 0.0)
                high, low = split(down)
                restrict[k * size:(k + 1) * size, s * size:(s + 1) * size] = high
                restrict[(2 + k) * size:(3 + k) * size, s * size:(s + 1) * size] = low
                up = jnp.where(targets[s, 1] == k, links[s, 1], 0.0)
                high, low = split(up)
                prolong[s * size:(s + 1) * size, k * size:(k + 1) * size] = high
                prolong[(slots + s) * size:(slots + s + 1) * size, k * size:(k + 1) * size] = low
        right = split_columns(rhs[...].reshape(slots * size, size))
        mids[...] = product(restrict[...], right).reshape(mids.shape)

    @pl.when(lax.axis_index("lvl") != 0)
    def _():
        payload[0] = links[0, 0]
        payload[1] = links[2, 0]
        payload[2] = jnp.zeros_like(payload[2])
        mids[...] = jnp.zeros_like(mids)


def operator_kernel(columns, tiles, matrix, gathered):
    slots, count, size = tiles.shape[0], tiles.shape[1], tiles.shape[-1]
    row = lax.axis_index("row")
    odd = lax.rem(row, 2)
    inner = (row > 0) & (row < lax.axis_size("row") - 1)
    gathered[...] = jnp.zeros_like(gathered)
    for s in range(slots):
        for j in range(count):
            code = columns[s, j]
            step = code // slots
            slot = code - slots * step
            side = jnp.where(step == 1, 0, jnp.where(step == 2 * (1 - odd), 1, 2))
            gathered[s, side * slots + slot] += tiles[s, j]
    for s in range(slots):
        for c in range(3 * slots):
            block = gathered[s, c]
            if c >= 2 * slots:
                block = jnp.where(inner, block, 0.0)
            high, low = split(block)
            matrix[s * size:(s + 1) * size, c * size:(c + 1) * size] = high
            matrix[(slots + s) * size:(slots + s + 1) * size, c * size:(c + 1) * size] = low


def load(field, refs):
    size = field.shape[0] // (len(refs) * refs[0].shape[0])
    for g, ref in enumerate(refs):
        for s in range(ref.shape[0]):
            high, low = split(ref[s])
            at = (g * ref.shape[0] + s) * size
            field[at:at + size, :size] = high
            field[at:at + size, size:] = low


def first_kernel(matrix, own, core, cross, down_own, down_core, down_cross, mid_own, mid_core, mid_cross, level, first, field):
    size = own.shape[-1]

    @pl.when(lax.axis_index("lvl") == 0)
    def _():
        load(field, (own, core, cross))
        level[...] = own[...]

    @pl.when(lax.axis_index("lvl") != 0)
    def _():
        for g, (down, mid) in enumerate(((down_own, mid_own), (down_core, mid_core), (down_cross, mid_cross))):
            left = split_rows(jnp.concatenate([down[0], down[1]], axis=1))
            right = split_columns(stacked(mid[0], mid[1]))
            coarse = product(left, right) + 0.5 * (mid[0] + mid[1])
            for s, value in enumerate((mid[0], coarse, mid[1])):
                high, low = split(value)
                at = (3 * g + s) * size
                field[at:at + size, :size] = high
                field[at:at + size, size:] = low
                if g == 0:
                    level[s] = value

    first[...] = product(matrix[...], field[...]).reshape(first.shape)


def second_kernel(matrix, level, own, core, cross, links, smooth, fixes, field):
    load(field, (own, core, cross))
    second = product(matrix[...], field[...]).reshape(level.shape)
    value = COEF_ZERO * level[...] + COEF_ONE * own[...] + COEF_TWO * second

    @pl.when(lax.axis_index("lvl") == 0)
    def _():
        smooth[...] = value
        fixes[...] = jnp.zeros_like(fixes)

    @pl.when(lax.axis_index("lvl") != 0)
    def _():
        coarse = value[1]
        up = product(split_rows(stacked(links[0, 1], links[2, 1])), split_columns(coarse))
        size = coarse.shape[0]
        low, high = value[0] + up[:size], value[2] + up[size:]
        smooth[0] = low
        smooth[1] = coarse
        smooth[2] = high
        fixes[0] = low + coarse
        fixes[1] = high + coarse


def solution_kernel(smooth, fixes, prolong, *rest):
    result = rest[-1]

    @pl.when(lax.axis_index("lvl") == 0)
    def _():
        right = split_columns(stacked(fixes[0], fixes[1]))
        value = smooth[...] + product(prolong[...], right).reshape(smooth.shape)
        if len(rest) == 2:
            value = value + rest[0][...]
        result[...] = value

    @pl.when(lax.axis_index("lvl") != 0)
    def _():
        result[...] = smooth[...]


def residual_kernel(matrix, own, core, cross, rhs, restrict, resid, mids, field):
    @pl.when(lax.axis_index("lvl") == 0)
    def _():
        load(field, (own, core, cross))
        value = rhs[...] - product(matrix[...], field[...]).reshape(rhs.shape)
        resid[...] = value
        right = split_columns(value.reshape(-1, value.shape[-1]))
        mids[...] = product(restrict[...], right).reshape(mids.shape)

    @pl.when(lax.axis_index("lvl") != 0)
    def _():
        resid[...] = jnp.zeros_like(resid)
        mids[...] = jnp.zeros_like(mids)


def call(kernel, outs, args, scalars=0, scratch=(), flops=0):
    spaces = [pl.BlockSpec(memory_space=pltpu.SMEM)] * scalars
    spaces += [pl.BlockSpec(memory_space=pltpu.VMEM)] * (len(args) - scalars)
    size = sum(a.size * a.dtype.itemsize for a in args)
    return pl.pallas_call(
        kernel,
        out_shape=[jax.ShapeDtypeStruct(shape, dtype) for shape, dtype in outs],
        in_specs=spaces,
        out_specs=[pl.BlockSpec(memory_space=pltpu.VMEM)] * len(outs),
        scratch_shapes=[pltpu.VMEM(shape, dtype) for shape, dtype in scratch],
        compiler_params=pltpu.CompilerParams(vmem_limit_bytes=24 * 1024 * 1024),
        cost_estimate=pl.CostEstimate(flops=flops, bytes_accessed=size, transcendentals=0),
    )(*args)


def swaps(rows):
    across = [0] + [r + 1 if r % 2 else r - 1 for r in range(1, rows - 1)] + [rows - 1]
    core = [(l * rows + r, l * rows + (r ^ 1)) for l in range(2) for r in range(rows)]
    cross = [(l * rows + r, l * rows + across[r]) for l in range(2) for r in range(1, rows - 1)]
    cross += [(l * rows + r, (1 - l) * rows + r) for l in range(2) for r in (0, rows - 1)]
    level = [(l * rows + r, (1 - l) * rows + r) for l in range(2) for r in range(rows)]
    skew = [(r, rows + across[r]) for r in range(rows)] + [(rows + r, r) for r in range(rows)]
    return tuple((lambda x, pairs=pairs: lax.ppermute(x, ("lvl", "row"), pairs)) for pairs in (core, cross, level, skew))


def paired(rhs, op_tiles, op_cols, link_tiles, level_links):
    core, cross, level, skew = swaps(lax.axis_size("row"))
    right, tiles, columns = rhs[0, 0], op_tiles[0, 0], op_cols[0, 0]
    links, targets = link_tiles[0, 0], level_links[0, 0]
    slots, size, width = right.shape
    blocks, pair = (right.shape, F32), ((2, size, width), F32)
    big, field = slots * size, ((3 * slots * size, 2 * width), BF16)
    mids, payload, restrict, prolong = call(
        restrict_kernel,
        [pair, blocks, ((4 * size, big), BF16), ((2 * big, 2 * size), BF16)],
        [targets, right, links],
        scalars=1,
    )
    down = None
    result = None
    matrix = None
    for cycle in range(CYCLES):
        if cycle > 0:
            resid, mids = call(
                residual_kernel,
                [blocks, pair],
                [matrix, result, core(result), cross(result), right, restrict],
                scratch=[field],
            )
            payload = resid
        mid_here, mid_cross = level(mids), skew(mids)
        around = (payload, core(payload), cross(payload))
        mid_core = core(mid_here)
        if cycle == 0:
            (matrix,) = call(
                operator_kernel,
                [((2 * big, 3 * big), BF16)],
                [columns, tiles],
                scalars=1,
                scratch=[((slots, 3 * slots, size, size), F32)],
            )
            down = around
        level_resid, first = call(
            first_kernel,
            [blocks, blocks],
            [matrix, *around, *down, mid_here, mid_core, mid_cross],
            scratch=[field],
        )
        smooth, fixes = call(
            second_kernel,
            [blocks, pair],
            [matrix, level_resid, first, core(first), cross(first), links],
            scratch=[field],
        )
        fixes = level(fixes)
        args = [smooth, fixes, prolong] + ([] if cycle == 0 else [result])
        (result,) = call(solution_kernel, [blocks], args)
    return result[None, None]


def solution(mesh):
    placed = (
        P("lvl", "row", None, None, None),
        P("lvl", "row", None, None, None, None),
        P("lvl", "row", None, None),
        P("lvl", "row", None, None, None, None),
        P("lvl", "row", None, None),
    )
    pairs = mesh.shape["lvl"] == 2 and mesh.shape["row"] % 2 == 0
    return jax.shard_map(
        paired if pairs else per_device,
        mesh=mesh,
        in_specs=placed,
        out_specs=P("lvl", "row", None, None, None),
        check_vma=False,
    )
```

```python
import functools

import jax
import jax.numpy as jnp
from jax import lax
from jax.experimental import pallas as pl
from jax.experimental.pallas import tpu as pltpu
from jax.sharding import PartitionSpec as P

CYCLES = 2


HIGH = lax.Precision.HIGHEST
COEF_ZERO = 0.9
COEF_ONE = -0.36
COEF_TWO = 0.05
F32 = jnp.float32
BF16 = jnp.bfloat16


def extended(block, sides, width):
    for axis, dim in sides:
        count = lax.axis_size(axis)
        forward = [(i, i + 1) for i in range(count - 1)]
        backward = [(target, source) for source, target in forward]
        low = lax.ppermute(
            lax.slice_in_dim(block, block.shape[dim] - width, None, axis=dim), axis, forward
        )
        high = lax.ppermute(lax.slice_in_dim(block, 0, width, axis=dim), axis, backward)
        block = jnp.concatenate([low, block, high], axis=dim)
    return block


def broadcast(block, axis, source):
    block = jnp.where(lax.axis_index(axis) == source, block, jnp.zeros_like(block))
    return lax.psum(block, axis)


def apply_operator(field, tiles, columns, keep):
    slots = field.shape[0]
    padded = extended(field[None], (("row", 0),), 1)
    candidates = padded.reshape((3 * slots,) + field.shape[1:])
    picked = candidates[columns]
    image = jnp.einsum("sjab,sjbn->san", tiles, picked, precision=HIGH)
    return image * keep[:, None, None]


def per_device(rhs, op_tiles, op_cols, link_tiles, level_links):
    n_lvl = lax.axis_size("lvl")
    fine_lvls = 5 * n_lvl // 8
    mid_lvls = max(n_lvl - fine_lvls - 1, 1)
    lvl_here = lax.axis_index("lvl")
    right = rhs[0, 0]
    tiles = op_tiles[0, 0]
    columns = op_cols[0, 0]
    links = link_tiles[0, 0]
    targets = level_links[0, 0]
    slots = right.shape[0]
    slot_ids = jnp.arange(slots)
    pair_ids = jnp.arange(2)
    is_fine = lvl_here < fine_lvls
    is_mid = (lvl_here >= fine_lvls) & (lvl_here < fine_lvls + mid_lvls)
    is_coarse = lvl_here == n_lvl - 1
    fine_keep = jnp.where(is_fine & (slot_ids >= 0), 1.0, 0.0).astype(jnp.float32)
    mid_keep = jnp.where(is_mid & ((slot_ids == 0) | (slot_ids == 2)), 1.0, 0.0).astype(jnp.float32)
    coarse_keep = jnp.where(is_coarse & (slot_ids == 1), 1.0, 0.0).astype(jnp.float32)
    all_keep = fine_keep + mid_keep + coarse_keep
    mid_flag = jnp.where(is_mid, 1.0, 0.0).astype(jnp.float32)
    place = (slot_ids[:, None] == 2 * pair_ids[None, :]).astype(jnp.float32) * mid_flag
    lvl_ids = jnp.arange(n_lvl)

    def lvl_table(target):
        by_lvl = (target[:, None] // 2 + fine_lvls == lvl_ids[None, :]).astype(jnp.float32)
        by_pair = (target[:, None] % 2 == pair_ids[None, :]).astype(jnp.float32)
        return by_lvl[:, :, None] * by_pair[:, None, :] * fine_keep[:, None, None]

    to_lvl = lvl_table(targets[:, 0])
    from_lvl = lvl_table(targets[:, 1])
    mid_restrict = jnp.stack([links[0, 0], links[2, 0]])
    mid_prolong = jnp.stack([links[0, 1], links[2, 1]])
    solution = jnp.zeros_like(right)
    mid_fix = jnp.zeros((2,) + right.shape[1:], jnp.float32)
    coarse_fix = jnp.zeros_like(right[0])
    for cycle in range(CYCLES):
        if cycle == 0:
            resid = right * fine_keep[:, None, None]
        else:
            resid = (right - apply_operator(solution, tiles, columns, all_keep)) * fine_keep[
                :, None, None
            ]
        terms = jnp.einsum("sab,sbn->san", links[:, 0], resid, precision=HIGH)
        dense = jnp.einsum("slm,san->lman", to_lvl, terms, precision=HIGH)
        mid_resid = lax.psum_scatter(dense, "lvl", scatter_dimension=0, tiled=True)[0] * mid_flag
        mid_part = jnp.einsum("mab,mbn->an", mid_restrict, mid_resid, precision=HIGH) * mid_flag
        fine_part = 0.5 * jnp.sum(terms * fine_keep[:, None, None], axis=0)
        coarse_resid = lax.psum(mid_part + fine_part, "lvl")
        level_resid = resid + jnp.einsum("sm,man->san", place, mid_resid, precision=HIGH)
        level_resid = level_resid + coarse_keep[:, None, None] * coarse_resid[None]
        first = apply_operator(level_resid, tiles, columns, all_keep)
        second = apply_operator(first, tiles, columns, all_keep)
        smooth = COEF_ZERO * level_resid + COEF_ONE * first + COEF_TWO * second
        coarse_fix = broadcast(smooth[1], "lvl", n_lvl - 1)
        mid_fix = jnp.stack([smooth[0], smooth[2]]) + jnp.einsum(
            "mab,bn->man", mid_prolong, coarse_fix, precision=HIGH
        )
        gathered = lax.all_gather(mid_fix[None], "lvl", axis=0, tiled=True)
        chosen = jnp.einsum("slm,lman->san", from_lvl, gathered, precision=HIGH)
        chosen = chosen + coarse_fix[None]
        fine_fix = smooth + jnp.einsum("sab,sbn->san", links[:, 1], chosen, precision=HIGH)
        solution = solution + fine_fix * fine_keep[:, None, None]
    levels = solution * fine_keep[:, None, None] + jnp.einsum(
        "sm,man->san", place, mid_fix, precision=HIGH
    )
    levels = levels + coarse_keep[:, None, None] * coarse_fix[None]
    return levels[None, None]


def split(value):
    high = value.astype(BF16)
    return high, (value - high.astype(F32)).astype(BF16)


def split_rows(value):
    return jnp.concatenate(split(value), axis=0)


def split_columns(value):
    return jnp.concatenate(split(value), axis=1)


def product(left, right):
    full = jnp.dot(left, right, preferred_element_type=F32)
    rows, columns = full.shape[0] // 2, full.shape[1] // 2
    small = full[rows:, :columns] + full[:rows, columns:] + full[rows:, columns:]
    return full[:rows, :columns] + small


def stacked(*blocks):
    return jnp.concatenate(blocks, axis=0)


def restrict_kernel(targets_in, rhs_in, links_in, mids, payload, restrict, targets, links, sems):
    size = payload.shape[-1]
    slots = payload.shape[0]
    fetch_targets = pltpu.make_async_copy(targets_in.at[0, 0], targets, sems.at[0])
    fetch_links = pltpu.make_async_copy(links_in, links, sems.at[1])
    fetch_rhs = pltpu.make_async_copy(rhs_in, payload, sems.at[2])
    fetch_targets.start()
    fetch_links.start()

    @pl.when(lax.axis_index("lvl") == 0)
    def _():
        fetch_rhs.start()
        fetch_targets.wait()
        fetch_links.wait()
        for s in range(slots):
            for k in range(2):
                down = jnp.where(targets[0, s] == k, links[s, 0], 0.0)
                high, low = split(down)
                restrict[k * size:(k + 1) * size, s * size:(s + 1) * size] = high
                restrict[(2 + k) * size:(3 + k) * size, s * size:(s + 1) * size] = low
        fetch_rhs.wait()
        right = split_columns(payload[...].reshape(slots * size, size))
        mids[...] = product(restrict[...], right).reshape(mids.shape)

    @pl.when(lax.axis_index("lvl") != 0)
    def _():
        fetch_targets.wait()
        fetch_links.wait()
        payload[0] = links[0, 0]
        payload[1] = links[2, 0]
        payload[2] = jnp.zeros_like(payload[2])
        mids[...] = jnp.zeros_like(mids)


def operator_kernel(columns_in, targets_in, links_in, tiles_in, matrix, prolong, columns, targets, links, tiles, gathered, sems):
    slots, count, size = tiles.shape[0], tiles.shape[1], tiles.shape[-1]
    fetch_columns = pltpu.make_async_copy(columns_in.at[0], columns, sems.at[0])
    fetch_targets = pltpu.make_async_copy(targets_in.at[0, 0], targets, sems.at[1])
    fetch_links = pltpu.make_async_copy(links_in, links, sems.at[2])
    fetch_tiles = [pltpu.make_async_copy(tiles_in.at[s], tiles.at[s], sems.at[3 + s]) for s in range(slots)]
    for fetch in (fetch_columns, fetch_targets, *fetch_tiles, fetch_links):
        fetch.start()
    row = lax.axis_index("row")
    odd = lax.rem(row, 2)
    inner = (row > 0) & (row < lax.axis_size("row") - 1)
    gathered[...] = jnp.zeros_like(gathered)
    fetch_columns.wait()
    fetch_targets.wait()
    for s in range(slots):
        fetch_tiles[s].wait()
        for j in range(count):
            code = columns[s, 0, j]
            step = code // slots
            slot = code - slots * step
            side = jnp.where(step == 1, 0, jnp.where(step == 2 * (1 - odd), 1, 2))
            gathered[s, side * slots + slot] += tiles[s, j]
        for c in range(3 * slots):
            block = gathered[s, c]
            if c >= 2 * slots:
                block = jnp.where(inner, block, 0.0)
            high, low = split(block)
            matrix[s * size:(s + 1) * size, c * size:(c + 1) * size] = high
            matrix[(slots + s) * size:(slots + s + 1) * size, c * size:(c + 1) * size] = low
    fetch_links.wait()
    for s in range(slots):
        for k in range(2):
            up = jnp.where(targets[1, s] == k, links[s, 1], 0.0)
            high, low = split(up)
            prolong[s * size:(s + 1) * size, k * size:(k + 1) * size] = high
            prolong[(slots + s) * size:(slots + s + 1) * size, k * size:(k + 1) * size] = low


def joined(blocks):
    return split_columns(stacked(*blocks))


def blocks_of(*refs):
    return [ref[s] for ref in refs for s in range(ref.shape[0])]


def near(matrix, field):
    columns = 2 * (matrix.shape[1] // 3)
    return product(matrix[:, :columns], field)


def far(matrix, field):
    columns = 2 * (matrix.shape[1] // 3)
    return product(matrix[:, columns:], field)


def level_blocks(down, mid):
    left = split_rows(jnp.concatenate([down[0], down[1]], axis=1))
    coarse = product(left, joined((mid[0], mid[1]))) + 0.5 * (mid[0] + mid[1])
    return [mid[0], coarse, mid[1]]


def first_kernel(matrix, own, core, cross, down_own, down_core, down_cross, mid_own, mid_core, mid_cross, level, first, field):
    @pl.when(lax.axis_index("lvl") == 0)
    def _():
        field[...] = joined(blocks_of(own, core, cross))
        level[...] = own[...]

    @pl.when(lax.axis_index("lvl") != 0)
    def _():
        here = level_blocks(down_own, mid_own)
        field[...] = joined(here + level_blocks(down_core, mid_core) + level_blocks(down_cross, mid_cross))
        level[...] = stacked(*here).reshape(level.shape)

    first[...] = product(matrix[...], field[...]).reshape(first.shape)


def near_kernel(matrix, own, core, core_last, part):
    part[...] = near(matrix, joined(blocks_of(own, core, core_last))).reshape(part.shape)


def second_kernel(matrix, level, own, part, cross, links, smooth, fixes):
    second = part[...] + far(matrix, joined(blocks_of(cross))).reshape(part.shape)
    value = COEF_ZERO * level[...] + COEF_ONE * own[...] + COEF_TWO * second

    @pl.when(lax.axis_index("lvl") == 0)
    def _():
        smooth[...] = value
        fixes[...] = jnp.zeros_like(fixes)

    @pl.when(lax.axis_index("lvl") != 0)
    def _():
        coarse = value[1]
        up = product(split_rows(stacked(links[0, 1], links[2, 1])), split_columns(coarse))
        size = coarse.shape[0]
        low, high = value[0] + up[:size], value[2] + up[size:]
        smooth[0] = low
        smooth[1] = coarse
        smooth[2] = high
        fixes[0] = low + coarse
        fixes[1] = high + coarse


def solution_kernel(smooth, fixes, prolong, *rest):
    result = rest[-1]

    @pl.when(lax.axis_index("lvl") == 0)
    def _():
        value = smooth[...] + product(prolong[...], joined((fixes[0], fixes[1]))).reshape(smooth.shape)
        if len(rest) == 2:
            value = value + rest[0][...]
        result[...] = value

    @pl.when(lax.axis_index("lvl") != 0)
    def _():
        result[...] = smooth[...]


def residual_kernel(matrix, part, cross, rhs, restrict, resid, mids):
    @pl.when(lax.axis_index("lvl") == 0)
    def _():
        value = rhs[...] - (part[...] + far(matrix, joined(blocks_of(cross))).reshape(rhs.shape))
        resid[...] = value
        mids[...] = product(restrict[...], joined([value[s] for s in range(value.shape[0])])).reshape(mids.shape)

    @pl.when(lax.axis_index("lvl") != 0)
    def _():
        resid[...] = jnp.zeros_like(resid)
        mids[...] = jnp.zeros_like(mids)


def call(kernel, outs, args, anywhere=0, scratch=(), aliases={}):
    args = [pltpu.with_memory_space_constraint(a, pltpu.HBM) for a in args[:anywhere]] + list(args[anywhere:])
    spaces = [pl.BlockSpec(memory_space=pltpu.HBM)] * anywhere
    spaces += [pl.BlockSpec(memory_space=pltpu.VMEM)] * (len(args) - anywhere)
    return pl.pallas_call(
        kernel,
        out_shape=[jax.ShapeDtypeStruct(shape, dtype) for shape, dtype in outs],
        in_specs=spaces,
        out_specs=[pl.BlockSpec(memory_space=pltpu.VMEM)] * len(outs),
        scratch_shapes=scratch,
        input_output_aliases=aliases,
        compiler_params=pltpu.CompilerParams(vmem_limit_bytes=24 * 1024 * 1024),
        cost_estimate=pl.CostEstimate(flops=0, bytes_accessed=0, transcendentals=0),
    )(*args)


def swaps(rows):
    across = [0] + [r + 1 if r % 2 else r - 1 for r in range(1, rows - 1)] + [rows - 1]
    core = [(l * rows + r, l * rows + (r ^ 1)) for l in range(2) for r in range(rows)]
    cross = [(l * rows + r, l * rows + across[r]) for l in range(2) for r in range(1, rows - 1)]
    cross += [(l * rows + r, (1 - l) * rows + r) for l in range(2) for r in (0, rows - 1)]
    fine = [(r, across[r]) for r in range(1, rows - 1)] + [(rows + r, rows + (r ^ 1)) for r in range(2, rows - 2)]
    for end, beside in ((0, 1), (rows - 1, rows - 2)):
        fine += [(end, rows + end), (rows + end, rows + beside), (rows + beside, end)]
    level = [(l * rows + r, (1 - l) * rows + r) for l in range(2) for r in range(rows)]
    skew = [(r, rows + across[r]) for r in range(rows)] + [(rows + r, r) for r in range(rows)]
    return tuple((lambda x, pairs=pairs: lax.ppermute(x, ("lvl", "row"), pairs)) for pairs in (core, cross, fine, level, skew))


def paired(rhs, op_tiles, op_cols, link_tiles, level_links):
    core, cross, fine, level, skew = swaps(lax.axis_size("row"))
    right, tiles, links = rhs[0, 0], op_tiles[0, 0], link_tiles[0, 0]
    slots, size, width = right.shape
    blocks, pair = (right.shape, F32), ((2, size, width), F32)
    big = slots * size
    codes, goals = jnp.swapaxes(op_cols, 1, 2), jnp.swapaxes(level_links, 2, 3)
    mids, payload, restrict = call(
        restrict_kernel,
        [pair, blocks, ((4 * size, big), BF16)],
        [goals, right, links],
        anywhere=3,
        scratch=[
            pltpu.SMEM(goals.shape[2:], goals.dtype),
            pltpu.VMEM(links.shape, links.dtype),
            pltpu.SemaphoreType.DMA((3,)),
        ],
    )
    down = result = matrix = prolong = None
    for cycle in range(CYCLES):
        if cycle > 0:
            result_cross = cross(result)
            (part,) = call(near_kernel, [blocks], [matrix, result, core(result[:-1]), core(result[-1:])])
            payload, mids = call(residual_kernel, [blocks, pair], [matrix, part, result_cross, right, restrict])
        mid_here, mid_cross = level(mids), skew(mids)
        around = (payload, core(payload), cross(payload) if cycle == 0 else fine(payload))
        mid_core = core(mid_here)
        if cycle == 0:
            matrix, prolong = call(
                operator_kernel,
                [((2 * big, 3 * big), BF16), ((2 * big, 2 * size), BF16)],
                [codes, goals, links, tiles],
                anywhere=4,
                scratch=[
                    pltpu.SMEM(codes.shape[1:], codes.dtype),
                    pltpu.SMEM(goals.shape[2:], goals.dtype),
                    pltpu.VMEM(links.shape, links.dtype),
                    pltpu.VMEM(tiles.shape, tiles.dtype),
                    pltpu.VMEM((slots, 3 * slots, size, size), F32),
                    pltpu.SemaphoreType.DMA((3 + slots,)),
                ],
            )
            down = around
        level_resid, first = call(
            first_kernel,
            [blocks, blocks],
            [matrix, *around, *down, mid_here, mid_core, mid_cross],
            scratch=[pltpu.VMEM((3 * big, 2 * width), BF16)],
        )
        first_cross = cross(first)
        (part,) = call(near_kernel, [blocks], [matrix, first, core(first[:-1]), core(first[-1:])])
        smooth, fixes = call(second_kernel, [blocks, pair], [matrix, level_resid, first, part, first_cross, links])
        fixes = level(fixes)
        args = [smooth, fixes, prolong] + ([] if cycle == 0 else [result])
        (result,) = call(solution_kernel, [blocks], args)
    return result[None, None]


def solution(mesh):
    placed = (
        P("lvl", "row", None, None, None),
        P("lvl", "row", None, None, None, None),
        P("lvl", "row", None, None),
        P("lvl", "row", None, None, None, None),
        P("lvl", "row", None, None),
    )
    pairs = mesh.shape["lvl"] == 2 and mesh.shape["row"] % 2 == 0
    return jax.shard_map(
        paired if pairs else per_device,
        mesh=mesh,
        in_specs=placed,
        out_specs=P("lvl", "row", None, None, None),
        check_vma=False,
    )
```

```python
import functools

import jax
import jax.numpy as jnp
from jax import lax
from jax.experimental import pallas as pl
from jax.experimental.pallas import tpu as pltpu
from jax.sharding import PartitionSpec as P

CYCLES = 2


HIGH = lax.Precision.HIGHEST
COEF_ZERO = 0.9
COEF_ONE = -0.36
COEF_TWO = 0.05
F32 = jnp.float32
BF16 = jnp.bfloat16


def extended(block, sides, width):
    for axis, dim in sides:
        count = lax.axis_size(axis)
        forward = [(i, i + 1) for i in range(count - 1)]
        backward = [(target, source) for source, target in forward]
        low = lax.ppermute(
            lax.slice_in_dim(block, block.shape[dim] - width, None, axis=dim), axis, forward
        )
        high = lax.ppermute(lax.slice_in_dim(block, 0, width, axis=dim), axis, backward)
        block = jnp.concatenate([low, block, high], axis=dim)
    return block


def broadcast(block, axis, source):
    block = jnp.where(lax.axis_index(axis) == source, block, jnp.zeros_like(block))
    return lax.psum(block, axis)


def apply_operator(field, tiles, columns, keep):
    slots = field.shape[0]
    padded = extended(field[None], (("row", 0),), 1)
    candidates = padded.reshape((3 * slots,) + field.shape[1:])
    picked = candidates[columns]
    image = jnp.einsum("sjab,sjbn->san", tiles, picked, precision=HIGH)
    return image * keep[:, None, None]


def per_device(rhs, op_tiles, op_cols, link_tiles, level_links):
    n_lvl = lax.axis_size("lvl")
    fine_lvls = 5 * n_lvl // 8
    mid_lvls = max(n_lvl - fine_lvls - 1, 1)
    lvl_here = lax.axis_index("lvl")
    right = rhs[0, 0]
    tiles = op_tiles[0, 0]
    columns = op_cols[0, 0]
    links = link_tiles[0, 0]
    targets = level_links[0, 0]
    slots = right.shape[0]
    slot_ids = jnp.arange(slots)
    pair_ids = jnp.arange(2)
    is_fine = lvl_here < fine_lvls
    is_mid = (lvl_here >= fine_lvls) & (lvl_here < fine_lvls + mid_lvls)
    is_coarse = lvl_here == n_lvl - 1
    fine_keep = jnp.where(is_fine & (slot_ids >= 0), 1.0, 0.0).astype(jnp.float32)
    mid_keep = jnp.where(is_mid & ((slot_ids == 0) | (slot_ids == 2)), 1.0, 0.0).astype(jnp.float32)
    coarse_keep = jnp.where(is_coarse & (slot_ids == 1), 1.0, 0.0).astype(jnp.float32)
    all_keep = fine_keep + mid_keep + coarse_keep
    mid_flag = jnp.where(is_mid, 1.0, 0.0).astype(jnp.float32)
    place = (slot_ids[:, None] == 2 * pair_ids[None, :]).astype(jnp.float32) * mid_flag
    lvl_ids = jnp.arange(n_lvl)

    def lvl_table(target):
        by_lvl = (target[:, None] // 2 + fine_lvls == lvl_ids[None, :]).astype(jnp.float32)
        by_pair = (target[:, None] % 2 == pair_ids[None, :]).astype(jnp.float32)
        return by_lvl[:, :, None] * by_pair[:, None, :] * fine_keep[:, None, None]

    to_lvl = lvl_table(targets[:, 0])
    from_lvl = lvl_table(targets[:, 1])
    mid_restrict = jnp.stack([links[0, 0], links[2, 0]])
    mid_prolong = jnp.stack([links[0, 1], links[2, 1]])
    solution = jnp.zeros_like(right)
    mid_fix = jnp.zeros((2,) + right.shape[1:], jnp.float32)
    coarse_fix = jnp.zeros_like(right[0])
    for cycle in range(CYCLES):
        if cycle == 0:
            resid = right * fine_keep[:, None, None]
        else:
            resid = (right - apply_operator(solution, tiles, columns, all_keep)) * fine_keep[
                :, None, None
            ]
        terms = jnp.einsum("sab,sbn->san", links[:, 0], resid, precision=HIGH)
        dense = jnp.einsum("slm,san->lman", to_lvl, terms, precision=HIGH)
        mid_resid = lax.psum_scatter(dense, "lvl", scatter_dimension=0, tiled=True)[0] * mid_flag
        mid_part = jnp.einsum("mab,mbn->an", mid_restrict, mid_resid, precision=HIGH) * mid_flag
        fine_part = 0.5 * jnp.sum(terms * fine_keep[:, None, None], axis=0)
        coarse_resid = lax.psum(mid_part + fine_part, "lvl")
        level_resid = resid + jnp.einsum("sm,man->san", place, mid_resid, precision=HIGH)
        level_resid = level_resid + coarse_keep[:, None, None] * coarse_resid[None]
        first = apply_operator(level_resid, tiles, columns, all_keep)
        second = apply_operator(first, tiles, columns, all_keep)
        smooth = COEF_ZERO * level_resid + COEF_ONE * first + COEF_TWO * second
        coarse_fix = broadcast(smooth[1], "lvl", n_lvl - 1)
        mid_fix = jnp.stack([smooth[0], smooth[2]]) + jnp.einsum(
            "mab,bn->man", mid_prolong, coarse_fix, precision=HIGH
        )
        gathered = lax.all_gather(mid_fix[None], "lvl", axis=0, tiled=True)
        chosen = jnp.einsum("slm,lman->san", from_lvl, gathered, precision=HIGH)
        chosen = chosen + coarse_fix[None]
        fine_fix = smooth + jnp.einsum("sab,sbn->san", links[:, 1], chosen, precision=HIGH)
        solution = solution + fine_fix * fine_keep[:, None, None]
    levels = solution * fine_keep[:, None, None] + jnp.einsum(
        "sm,man->san", place, mid_fix, precision=HIGH
    )
    levels = levels + coarse_keep[:, None, None] * coarse_fix[None]
    return levels[None, None]


def split(value):
    high = value.astype(BF16)
    return high, (value - high.astype(F32)).astype(BF16)


def split_rows(value):
    return jnp.concatenate(split(value), axis=0)


def split_columns(value):
    return jnp.concatenate(split(value), axis=1)


def product(left, right):
    full = jnp.dot(left, right, preferred_element_type=F32)
    rows, columns = full.shape[0] // 2, full.shape[1] // 2
    small = full[rows:, :columns] + full[:rows, columns:] + full[rows:, columns:]
    return full[:rows, :columns] + small


def stacked(*blocks):
    return jnp.concatenate(blocks, axis=0)


def store_mids(value, mids, skewed):
    mids[...] = value.reshape(mids.shape)
    skewed[:value.shape[0], :] = value
    skewed[value.shape[0]:, :] = jnp.zeros_like(skewed[value.shape[0]:, :])


def restrict_kernel(targets_in, rhs_in, links_in, mids, skewed, payload, restrict, targets, links, sems):
    size = payload.shape[-1]
    slots = payload.shape[0]
    fetch_targets = pltpu.make_async_copy(targets_in.at[0, 0], targets, sems.at[0])
    fetch_links = pltpu.make_async_copy(links_in, links, sems.at[1])
    fetch_rhs = pltpu.make_async_copy(rhs_in, payload, sems.at[2])
    fetch_targets.start()
    fetch_links.start()

    @pl.when(lax.axis_index("lvl") == 0)
    def _():
        fetch_rhs.start()
        fetch_targets.wait()
        fetch_links.wait()
        for s in range(slots):
            for k in range(2):
                down = jnp.where(targets[0, s] == k, links[s, 0], 0.0)
                high, low = split(down)
                restrict[k * size:(k + 1) * size, s * size:(s + 1) * size] = high
                restrict[(2 + k) * size:(3 + k) * size, s * size:(s + 1) * size] = low
        fetch_rhs.wait()
        right = split_columns(payload[...].reshape(slots * size, size))
        store_mids(product(restrict[...], right), mids, skewed)

    @pl.when(lax.axis_index("lvl") != 0)
    def _():
        fetch_targets.wait()
        fetch_links.wait()
        payload[0] = links[0, 0]
        payload[1] = links[2, 0]
        payload[2] = jnp.zeros_like(payload[2])
        mids[...] = jnp.zeros_like(mids)
        skewed[...] = jnp.zeros_like(skewed)


def operator_kernel(columns_in, targets_in, links_in, tiles_in, matrix, prolong, columns, targets, links, tiles, gathered, sems):
    slots, count, size = tiles.shape[0], tiles.shape[1], tiles.shape[-1]
    fetch_columns = pltpu.make_async_copy(columns_in.at[0], columns, sems.at[0])
    fetch_targets = pltpu.make_async_copy(targets_in.at[0, 0], targets, sems.at[1])
    fetch_links = pltpu.make_async_copy(links_in, links, sems.at[2])
    fetch_tiles = [pltpu.make_async_copy(tiles_in.at[s], tiles.at[s], sems.at[3 + s]) for s in range(slots)]
    for fetch in (fetch_columns, fetch_targets, *fetch_tiles, fetch_links):
        fetch.start()
    row = lax.axis_index("row")
    odd = lax.rem(row, 2)
    inner = (row > 0) & (row < lax.axis_size("row") - 1)
    gathered[...] = jnp.zeros_like(gathered)
    fetch_columns.wait()
    fetch_targets.wait()
    for s in range(slots):
        fetch_tiles[s].wait()
        for j in range(count):
            code = columns[s, 0, j]
            step = code // slots
            slot = code - slots * step
            side = jnp.where(step == 1, 0, jnp.where(step == 2 * (1 - odd), 1, 2))
            gathered[s, side * slots + slot] += tiles[s, j]
        for c in range(3 * slots):
            block = gathered[s, c]
            if c >= 2 * slots:
                block = jnp.where(inner, block, 0.0)
            high, low = split(block)
            matrix[s * size:(s + 1) * size, c * size:(c + 1) * size] = high
            matrix[(slots + s) * size:(slots + s + 1) * size, c * size:(c + 1) * size] = low
    fetch_links.wait()
    for s in range(slots):
        for k in range(2):
            up = jnp.where(targets[1, s] == k, links[s, 1], 0.0)
            high, low = split(up)
            prolong[s * size:(s + 1) * size, k * size:(k + 1) * size] = high
            prolong[(slots + s) * size:(slots + s + 1) * size, k * size:(k + 1) * size] = low


def joined(blocks):
    return split_columns(stacked(*blocks))


def blocks_of(*refs):
    return [ref[s] for ref in refs for s in range(ref.shape[0])]


def near(matrix, field):
    columns = 2 * (matrix.shape[1] // 3)
    return product(matrix[:, :columns], field)


def far(matrix, field):
    columns = 2 * (matrix.shape[1] // 3)
    return product(matrix[:, columns:], field)


def level_blocks(down, mid):
    left = split_rows(jnp.concatenate([down[0], down[1]], axis=1))
    coarse = product(left, joined((mid[0], mid[1]))) + 0.5 * (mid[0] + mid[1])
    return [mid[0], coarse, mid[1]]


def first_near_kernel(matrix, own, core, core_last, down_own, down_core, mid_own, mid_core, mid_core_last, level, part, field):
    @pl.when(lax.axis_index("lvl") == 0)
    def _():
        field[...] = joined(blocks_of(own, core, core_last))
        level[...] = own[...]

    @pl.when(lax.axis_index("lvl") != 0)
    def _():
        here = level_blocks(down_own, blocks_of(mid_own))
        field[...] = joined(here + level_blocks(down_core, blocks_of(mid_core, mid_core_last)))
        level[...] = stacked(*here).reshape(level.shape)

    part[...] = near(matrix, field[...]).reshape(part.shape)


def first_far_kernel(matrix, part, cross, down_cross, skewed, first, field):
    @pl.when(lax.axis_index("lvl") == 0)
    def _():
        field[...] = joined(blocks_of(cross))

    @pl.when(lax.axis_index("lvl") != 0)
    def _():
        size = cross.shape[-1]
        field[...] = joined(level_blocks(down_cross, (skewed[:size, :], skewed[size:2 * size, :])))

    first[...] = part[...] + far(matrix, field[...]).reshape(first.shape)


def near_kernel(matrix, own, core, core_last, part):
    part[...] = near(matrix, joined(blocks_of(own, core, core_last))).reshape(part.shape)


def second_kernel(matrix, level, own, part, cross, links, smooth, fixes):
    second = part[...] + far(matrix, joined(blocks_of(cross))).reshape(part.shape)
    value = COEF_ZERO * level[...] + COEF_ONE * own[...] + COEF_TWO * second

    @pl.when(lax.axis_index("lvl") == 0)
    def _():
        smooth[...] = value
        fixes[...] = jnp.zeros_like(fixes)

    @pl.when(lax.axis_index("lvl") != 0)
    def _():
        coarse = value[1]
        up = product(split_rows(stacked(links[0, 1], links[2, 1])), split_columns(coarse))
        size = coarse.shape[0]
        low, high = value[0] + up[:size], value[2] + up[size:]
        smooth[0] = low
        smooth[1] = coarse
        smooth[2] = high
        fixes[0] = low + coarse
        fixes[1] = high + coarse


def solution_kernel(smooth, fixes, prolong, *rest):
    result = rest[-1]

    @pl.when(lax.axis_index("lvl") == 0)
    def _():
        value = smooth[...] + product(prolong[...], joined((fixes[0], fixes[1]))).reshape(smooth.shape)
        if len(rest) == 2:
            value = value + rest[0][...]
        result[...] = value

    @pl.when(lax.axis_index("lvl") != 0)
    def _():
        result[...] = smooth[...]


def residual_kernel(matrix, part, cross, rhs, restrict, resid, mids, skewed):
    @pl.when(lax.axis_index("lvl") == 0)
    def _():
        value = rhs[...] - (part[...] + far(matrix, joined(blocks_of(cross))).reshape(rhs.shape))
        resid[...] = value
        store_mids(product(restrict[...], joined([value[s] for s in range(value.shape[0])])), mids, skewed)

    @pl.when(lax.axis_index("lvl") != 0)
    def _():
        resid[...] = jnp.zeros_like(resid)
        mids[...] = jnp.zeros_like(mids)
        skewed[...] = jnp.zeros_like(skewed)


def call(kernel, outs, args, anywhere=0, scratch=(), aliases={}):
    args = [pltpu.with_memory_space_constraint(a, pltpu.HBM) for a in args[:anywhere]] + list(args[anywhere:])
    spaces = [pl.BlockSpec(memory_space=pltpu.HBM)] * anywhere
    spaces += [pl.BlockSpec(memory_space=pltpu.VMEM)] * (len(args) - anywhere)
    return pl.pallas_call(
        kernel,
        out_shape=[jax.ShapeDtypeStruct(shape, dtype) for shape, dtype in outs],
        in_specs=spaces,
        out_specs=[pl.BlockSpec(memory_space=pltpu.VMEM)] * len(outs),
        scratch_shapes=scratch,
        input_output_aliases=aliases,
        compiler_params=pltpu.CompilerParams(vmem_limit_bytes=24 * 1024 * 1024),
        cost_estimate=pl.CostEstimate(flops=0, bytes_accessed=0, transcendentals=0),
    )(*args)


def swaps(rows):
    across = [0] + [r + 1 if r % 2 else r - 1 for r in range(1, rows - 1)] + [rows - 1]
    core = [(l * rows + r, l * rows + (r ^ 1)) for l in range(2) for r in range(rows)]
    cross = [(l * rows + r, l * rows + across[r]) for l in range(2) for r in range(1, rows - 1)]
    cross += [(l * rows + r, (1 - l) * rows + r) for l in range(2) for r in (0, rows - 1)]
    fine = [(r, across[r]) for r in range(1, rows - 1)] + [(rows + r, rows + (r ^ 1)) for r in range(2, rows - 2)]
    for end, beside in ((0, 1), (rows - 1, rows - 2)):
        fine += [(end, rows + end), (rows + end, rows + beside), (rows + beside, end)]
    level = [(l * rows + r, (1 - l) * rows + r) for l in range(2) for r in range(rows)]
    skew = [(r, rows + across[r]) for r in range(1, rows - 1)]
    skew += [(rows + r, r) for r in range(rows) if r not in (1, rows - 2)]
    for end, beside in ((0, 1), (rows - 1, rows - 2)):
        skew += [(end, beside), (rows + beside, rows + end)]
    return tuple((lambda x, pairs=pairs: lax.ppermute(x, ("lvl", "row"), pairs)) for pairs in (core, cross, fine, level, skew))


def paired(rhs, op_tiles, op_cols, link_tiles, level_links):
    core, cross, fine, level, skew = swaps(lax.axis_size("row"))
    right, tiles, links = rhs[0, 0], op_tiles[0, 0], link_tiles[0, 0]
    slots, size, width = right.shape
    blocks, pair = (right.shape, F32), ((2, size, width), F32)
    big = slots * size
    codes, goals = jnp.swapaxes(op_cols, 1, 2), jnp.swapaxes(level_links, 2, 3)
    long = ((2 * size + 8, width), F32)
    mids, skewed, payload, restrict = call(
        restrict_kernel,
        [pair, long, blocks, ((4 * size, big), BF16)],
        [goals, right, links],
        anywhere=3,
        scratch=[
            pltpu.SMEM(goals.shape[2:], goals.dtype),
            pltpu.VMEM(links.shape, links.dtype),
            pltpu.SemaphoreType.DMA((3,)),
        ],
    )
    down = result = matrix = prolong = None
    for cycle in range(CYCLES):
        if cycle > 0:
            result_cross = cross(result)
            (part,) = call(near_kernel, [blocks], [matrix, result, core(result[:-1]), core(result[-1:])])
            payload, mids, skewed = call(residual_kernel, [blocks, pair, long], [matrix, part, result_cross, right, restrict])
        mid_here, mid_cross = level(mids), skew(skewed)
        around = (payload, core(payload[:-1]), core(payload[-1:]), cross(payload) if cycle == 0 else fine(payload))
        mid_core = core(mid_here[:1]), core(mid_here[1:])
        if cycle == 0:
            matrix, prolong = call(
                operator_kernel,
                [((2 * big, 3 * big), BF16), ((2 * big, 2 * size), BF16)],
                [codes, goals, links, tiles],
                anywhere=4,
                scratch=[
                    pltpu.SMEM(codes.shape[1:], codes.dtype),
                    pltpu.SMEM(goals.shape[2:], goals.dtype),
                    pltpu.VMEM(links.shape, links.dtype),
                    pltpu.VMEM(tiles.shape, tiles.dtype),
                    pltpu.VMEM((slots, 3 * slots, size, size), F32),
                    pltpu.SemaphoreType.DMA((3 + slots,)),
                ],
            )
            down = around[0], around[1], around[3]
        level_resid, part = call(
            first_near_kernel,
            [blocks, blocks],
            [matrix, *around[:3], *down[:2], mid_here, *mid_core],
            scratch=[pltpu.VMEM((2 * big, 2 * width), BF16)],
        )
        (first,) = call(
            first_far_kernel,
            [blocks],
            [matrix, part, around[3], down[2], mid_cross],
            scratch=[pltpu.VMEM((big, 2 * width), BF16)],
        )
        first_cross = cross(first)
        (part,) = call(near_kernel, [blocks], [matrix, first, core(first[:-1]), core(first[-1:])])
        smooth, fixes = call(second_kernel, [blocks, pair], [matrix, level_resid, first, part, first_cross, links])
        fixes = level(fixes)
        args = [smooth, fixes, prolong] + ([] if cycle == 0 else [result])
        (result,) = call(solution_kernel, [blocks], args)
    return result[None, None]


def solution(mesh):
    placed = (
        P("lvl", "row", None, None, None),
        P("lvl", "row", None, None, None, None),
        P("lvl", "row", None, None),
        P("lvl", "row", None, None, None, None),
        P("lvl", "row", None, None),
    )
    pairs = mesh.shape["lvl"] == 2 and mesh.shape["row"] % 2 == 0
    return jax.shard_map(
        paired if pairs else per_device,
        mesh=mesh,
        in_specs=placed,
        out_specs=P("lvl", "row", None, None, None),
        check_vma=False,
    )
```

```python
import functools

import jax
import jax.numpy as jnp
from jax import lax
from jax.experimental import pallas as pl
from jax.experimental.pallas import tpu as pltpu
from jax.sharding import PartitionSpec as P

CYCLES = 2


HIGH = lax.Precision.HIGHEST
COEF_ZERO = 0.9
COEF_ONE = -0.36
COEF_TWO = 0.05
F32 = jnp.float32
BF16 = jnp.bfloat16


def extended(block, sides, width):
    for axis, dim in sides:
        count = lax.axis_size(axis)
        forward = [(i, i + 1) for i in range(count - 1)]
        backward = [(target, source) for source, target in forward]
        low = lax.ppermute(
            lax.slice_in_dim(block, block.shape[dim] - width, None, axis=dim), axis, forward
        )
        high = lax.ppermute(lax.slice_in_dim(block, 0, width, axis=dim), axis, backward)
        block = jnp.concatenate([low, block, high], axis=dim)
    return block


def broadcast(block, axis, source):
    block = jnp.where(lax.axis_index(axis) == source, block, jnp.zeros_like(block))
    return lax.psum(block, axis)


def apply_operator(field, tiles, columns, keep):
    slots = field.shape[0]
    padded = extended(field[None], (("row", 0),), 1)
    candidates = padded.reshape((3 * slots,) + field.shape[1:])
    picked = candidates[columns]
    image = jnp.einsum("sjab,sjbn->san", tiles, picked, precision=HIGH)
    return image * keep[:, None, None]


def per_device(rhs, op_tiles, op_cols, link_tiles, level_links):
    n_lvl = lax.axis_size("lvl")
    fine_lvls = 5 * n_lvl // 8
    mid_lvls = max(n_lvl - fine_lvls - 1, 1)
    lvl_here = lax.axis_index("lvl")
    right = rhs[0, 0]
    tiles = op_tiles[0, 0]
    columns = op_cols[0, 0]
    links = link_tiles[0, 0]
    targets = level_links[0, 0]
    slots = right.shape[0]
    slot_ids = jnp.arange(slots)
    pair_ids = jnp.arange(2)
    is_fine = lvl_here < fine_lvls
    is_mid = (lvl_here >= fine_lvls) & (lvl_here < fine_lvls + mid_lvls)
    is_coarse = lvl_here == n_lvl - 1
    fine_keep = jnp.where(is_fine & (slot_ids >= 0), 1.0, 0.0).astype(jnp.float32)
    mid_keep = jnp.where(is_mid & ((slot_ids == 0) | (slot_ids == 2)), 1.0, 0.0).astype(jnp.float32)
    coarse_keep = jnp.where(is_coarse & (slot_ids == 1), 1.0, 0.0).astype(jnp.float32)
    all_keep = fine_keep + mid_keep + coarse_keep
    mid_flag = jnp.where(is_mid, 1.0, 0.0).astype(jnp.float32)
    place = (slot_ids[:, None] == 2 * pair_ids[None, :]).astype(jnp.float32) * mid_flag
    lvl_ids = jnp.arange(n_lvl)

    def lvl_table(target):
        by_lvl = (target[:, None] // 2 + fine_lvls == lvl_ids[None, :]).astype(jnp.float32)
        by_pair = (target[:, None] % 2 == pair_ids[None, :]).astype(jnp.float32)
        return by_lvl[:, :, None] * by_pair[:, None, :] * fine_keep[:, None, None]

    to_lvl = lvl_table(targets[:, 0])
    from_lvl = lvl_table(targets[:, 1])
    mid_restrict = jnp.stack([links[0, 0], links[2, 0]])
    mid_prolong = jnp.stack([links[0, 1], links[2, 1]])
    solution = jnp.zeros_like(right)
    mid_fix = jnp.zeros((2,) + right.shape[1:], jnp.float32)
    coarse_fix = jnp.zeros_like(right[0])
    for cycle in range(CYCLES):
        if cycle == 0:
            resid = right * fine_keep[:, None, None]
        else:
            resid = (right - apply_operator(solution, tiles, columns, all_keep)) * fine_keep[
                :, None, None
            ]
        terms = jnp.einsum("sab,sbn->san", links[:, 0], resid, precision=HIGH)
        dense = jnp.einsum("slm,san->lman", to_lvl, terms, precision=HIGH)
        mid_resid = lax.psum_scatter(dense, "lvl", scatter_dimension=0, tiled=True)[0] * mid_flag
        mid_part = jnp.einsum("mab,mbn->an", mid_restrict, mid_resid, precision=HIGH) * mid_flag
        fine_part = 0.5 * jnp.sum(terms * fine_keep[:, None, None], axis=0)
        coarse_resid = lax.psum(mid_part + fine_part, "lvl")
        level_resid = resid + jnp.einsum("sm,man->san", place, mid_resid, precision=HIGH)
        level_resid = level_resid + coarse_keep[:, None, None] * coarse_resid[None]
        first = apply_operator(level_resid, tiles, columns, all_keep)
        second = apply_operator(first, tiles, columns, all_keep)
        smooth = COEF_ZERO * level_resid + COEF_ONE * first + COEF_TWO * second
        coarse_fix = broadcast(smooth[1], "lvl", n_lvl - 1)
        mid_fix = jnp.stack([smooth[0], smooth[2]]) + jnp.einsum(
            "mab,bn->man", mid_prolong, coarse_fix, precision=HIGH
        )
        gathered = lax.all_gather(mid_fix[None], "lvl", axis=0, tiled=True)
        chosen = jnp.einsum("slm,lman->san", from_lvl, gathered, precision=HIGH)
        chosen = chosen + coarse_fix[None]
        fine_fix = smooth + jnp.einsum("sab,sbn->san", links[:, 1], chosen, precision=HIGH)
        solution = solution + fine_fix * fine_keep[:, None, None]
    levels = solution * fine_keep[:, None, None] + jnp.einsum(
        "sm,man->san", place, mid_fix, precision=HIGH
    )
    levels = levels + coarse_keep[:, None, None] * coarse_fix[None]
    return levels[None, None]


def split(value):
    high = value.astype(BF16)
    return high, (value - high.astype(F32)).astype(BF16)


def split_rows(value):
    return jnp.concatenate(split(value), axis=0)


def split_columns(value):
    return jnp.concatenate(split(value), axis=1)


def product(left, right):
    full = jnp.dot(left, right, preferred_element_type=F32)
    rows, columns = full.shape[0] // 2, full.shape[1] // 2
    small = full[rows:, :columns] + full[:rows, columns:] + full[rows:, columns:]
    return full[:rows, :columns] + small


def stacked(*blocks):
    return jnp.concatenate(blocks, axis=0)


def store_mids(value, mids, skewed):
    mids[...] = value.reshape(mids.shape)
    skewed[:value.shape[0], :] = value
    skewed[value.shape[0]:, :] = jnp.zeros_like(skewed[value.shape[0]:, :])


def restrict_kernel(targets_in, rhs_in, links_in, mids, skewed, payload, wide, restrict, targets, links, sems):
    size = payload.shape[-1]
    slots = payload.shape[0]
    fetch_targets = pltpu.make_async_copy(targets_in.at[0, 0], targets, sems.at[0])
    fetch_links = pltpu.make_async_copy(links_in, links, sems.at[1])
    fetch_rhs = pltpu.make_async_copy(rhs_in, payload, sems.at[2])
    fetch_targets.start()
    fetch_links.start()

    @pl.when(lax.axis_index("lvl") == 0)
    def _():
        fetch_rhs.start()
        fetch_targets.wait()
        fetch_links.wait()
        for s in range(slots):
            for k in range(2):
                down = jnp.where(targets[0, s] == k, links[s, 0], 0.0)
                high, low = split(down)
                restrict[k * size:(k + 1) * size, s * size:(s + 1) * size] = high
                restrict[(2 + k) * size:(3 + k) * size, s * size:(s + 1) * size] = low
        fetch_rhs.wait()
        right = split_columns(payload[...].reshape(slots * size, size))
        store_mids(product(restrict[...], right), mids, skewed)
        wide[...] = jnp.zeros_like(wide)

    @pl.when(lax.axis_index("lvl") != 0)
    def _():
        fetch_targets.wait()
        fetch_links.wait()
        payload[0] = links[0, 0]
        payload[1] = links[2, 0]
        payload[2] = jnp.zeros_like(payload[2])
        wide[:2 * size, :] = stacked(links[0, 0], links[2, 0])
        wide[2 * size:, :] = jnp.zeros_like(wide[2 * size:, :])
        mids[...] = jnp.zeros_like(mids)
        skewed[...] = jnp.zeros_like(skewed)


def operator_kernel(columns_in, targets_in, links_in, tiles_in, matrix, prolong, columns, targets, links, tiles, gathered, sems):
    slots, count, size = tiles.shape[0], tiles.shape[1], tiles.shape[-1]
    fetch_columns = pltpu.make_async_copy(columns_in.at[0], columns, sems.at[0])
    fetch_targets = pltpu.make_async_copy(targets_in.at[0, 0], targets, sems.at[1])
    fetch_links = pltpu.make_async_copy(links_in, links, sems.at[2])
    fetch_tiles = [pltpu.make_async_copy(tiles_in.at[s], tiles.at[s], sems.at[3 + s]) for s in range(slots)]
    for fetch in (fetch_columns, fetch_targets, *fetch_tiles, fetch_links):
        fetch.start()
    row = lax.axis_index("row")
    odd = lax.rem(row, 2)
    inner = (row > 0) & (row < lax.axis_size("row") - 1)
    gathered[...] = jnp.zeros_like(gathered)
    fetch_columns.wait()
    fetch_targets.wait()
    for s in range(slots):
        fetch_tiles[s].wait()
        for j in range(count):
            code = columns[s, 0, j]
            step = code // slots
            slot = code - slots * step
            side = jnp.where(step == 1, 0, jnp.where(step == 2 * (1 - odd), 1, 2))
            gathered[s, side * slots + slot] += tiles[s, j]
        for c in range(3 * slots):
            block = gathered[s, c]
            if c >= 2 * slots:
                block = jnp.where(inner, block, 0.0)
            high, low = split(block)
            matrix[s * size:(s + 1) * size, c * size:(c + 1) * size] = high
            matrix[(slots + s) * size:(slots + s + 1) * size, c * size:(c + 1) * size] = low
    fetch_links.wait()

    @pl.when(lax.axis_index("lvl") == 0)
    def _():
        for s in range(slots):
            for k in range(2):
                up = jnp.where(targets[1, s] == k, links[s, 1], 0.0)
                high, low = split(up)
                prolong[s * size:(s + 1) * size, k * size:(k + 1) * size] = high
                prolong[(slots + s) * size:(slots + s + 1) * size, k * size:(k + 1) * size] = low

    @pl.when(lax.axis_index("lvl") != 0)
    def _():
        prolong[:4 * size, :size] = split_rows(stacked(links[0, 1], links[2, 1]))


def joined(blocks):
    return split_columns(stacked(*blocks))


def blocks_of(*refs):
    return [ref[s] for ref in refs for s in range(ref.shape[0])]


def own_slots(matrix, sides, groups):
    size = groups[0][0].shape[0]
    slots = len(groups[0])
    parts = []
    for s in range(slots):
        columns = [slice((side * slots + s) * size, (side * slots + s + 1) * size) for side in sides]
        high = [matrix[s * size:(s + 1) * size, c] for c in columns]
        low = [matrix[(slots + s) * size:(slots + s + 1) * size, c] for c in columns]
        left = stacked(jnp.concatenate(high, axis=1), jnp.concatenate(low, axis=1))
        parts.append(product(left, joined([group[s] for group in groups])))
    return stacked(*parts).reshape(slots, size, -1)


def near(matrix, field):
    columns = 2 * (matrix.shape[1] // 3)
    return product(matrix[:, :columns], field)


def far(matrix, field):
    columns = 2 * (matrix.shape[1] // 3)
    return product(matrix[:, columns:], field)


def level_blocks(down, mid):
    left = split_rows(jnp.concatenate([down[0], down[1]], axis=1))
    coarse = product(left, joined((mid[0], mid[1]))) + 0.5 * (mid[0] + mid[1])
    return [mid[0], coarse, mid[1]]


def rows_of(ref):
    size = ref.shape[-1]
    return [ref[k * size:(k + 1) * size, :] for k in range(2)]


def first_fine_kernel(matrix, own, core, core_last, part):
    @pl.when(lax.axis_index("lvl") == 0)
    def _():
        part[...] = near(matrix, joined(blocks_of(own, core, core_last))).reshape(part.shape)


def first_near_kernel(fine_part, matrix, own, down_own, down_core, mid_own, mid_core, mid_core_last, part, level):
    @pl.when(lax.axis_index("lvl") == 0)
    def _():
        level[...] = own[...]

    @pl.when(lax.axis_index("lvl") != 0)
    def _():
        here = level_blocks(down_own, blocks_of(mid_own))
        beside = level_blocks(down_core, blocks_of(mid_core, mid_core_last))
        level[...] = stacked(*here).reshape(level.shape)
        part[...] = own_slots(matrix, (0, 1), (here, beside))


def start_near_kernel(matrix, own, down_own, down_core, mid_own, mid_core, part, level):
    @pl.when(lax.axis_index("lvl") == 0)
    def _():
        level[...] = own[...]
        part[...] = near(matrix, joined(blocks_of(own, down_core))).reshape(part.shape)

    @pl.when(lax.axis_index("lvl") != 0)
    def _():
        here = level_blocks(down_own, blocks_of(mid_own))
        beside = level_blocks(down_core, blocks_of(mid_core))
        level[...] = stacked(*here).reshape(level.shape)
        part[...] = own_slots(matrix, (0, 1), (here, beside))


def start_far_kernel(matrix, part, cross, down_cross, skewed, first):
    @pl.when(lax.axis_index("lvl") == 0)
    def _():
        first[...] = part[...] + far(matrix, joined(blocks_of(cross))).reshape(first.shape)

    @pl.when(lax.axis_index("lvl") != 0)
    def _():
        beside = level_blocks(rows_of(down_cross), rows_of(skewed))
        first[...] = part[...] + own_slots(matrix, (2,), (beside,))


def first_far_kernel(matrix, part, cross, down_cross, skewed, first):
    @pl.when(lax.axis_index("lvl") == 0)
    def _():
        first[...] = part[...] + far(matrix, joined(blocks_of(cross))).reshape(first.shape)

    @pl.when(lax.axis_index("lvl") != 0)
    def _():
        beside = level_blocks(rows_of(down_cross), rows_of(skewed))
        first[...] = part[...] + own_slots(matrix, (2,), (beside,))


def near_kernel(matrix, own, core, core_last, part):
    @pl.when(lax.axis_index("lvl") == 0)
    def _():
        part[...] = near(matrix, joined(blocks_of(own, core, core_last))).reshape(part.shape)

    @pl.when(lax.axis_index("lvl") != 0)
    def _():
        part[...] = own_slots(matrix, (0, 1), (blocks_of(own), blocks_of(core, core_last)))


def second_kernel(matrix, level, own, part, cross, prolong, smooth, fixes):
    @pl.when(lax.axis_index("lvl") == 0)
    def _():
        second = part[...] + far(matrix, joined(blocks_of(cross))).reshape(part.shape)
        smooth[...] = COEF_ZERO * level[...] + COEF_ONE * own[...] + COEF_TWO * second
        fixes[...] = jnp.zeros_like(fixes)

    @pl.when(lax.axis_index("lvl") != 0)
    def _():
        second = part[...] + own_slots(matrix, (2,), (blocks_of(cross),))
        value = COEF_ZERO * level[...] + COEF_ONE * own[...] + COEF_TWO * second
        coarse = value[1]
        size = coarse.shape[0]
        up = product(prolong[:4 * size, :size], split_columns(coarse))
        low, high = value[0] + up[:size], value[2] + up[size:]
        smooth[0] = low
        smooth[1] = coarse
        smooth[2] = high
        fixes[0] = low + coarse
        fixes[1] = high + coarse


def solution_kernel(smooth, fixes, prolong, *rest):
    result = rest[-1]

    @pl.when(lax.axis_index("lvl") == 0)
    def _():
        value = smooth[...] + product(prolong[...], joined((fixes[0], fixes[1]))).reshape(smooth.shape)
        if len(rest) == 2:
            value = value + rest[0][...]
        result[...] = value

    @pl.when(lax.axis_index("lvl") != 0)
    def _():
        result[...] = smooth[...]


def tall_kernel(matrix, restrict, tall):
    big, wide = matrix.shape[0] // 2, restrict.shape[0] // 2

    @pl.when(lax.axis_index("lvl") == 0)
    def _():
        tall[:big, :] = matrix[:big, :]
        tall[big + wide:2 * big + wide, :] = matrix[big:, :]
        for c in range(0, matrix.shape[1], big):
            right = jnp.concatenate([matrix[:big, c:c + big], matrix[big:, c:c + big]], axis=1)
            high, low = split(product(restrict[...], right))
            tall[big:big + wide, c:c + big] = high
            tall[2 * big + wide:, c:c + big] = low


def residual_near_kernel(tall, own, core, core_last, part):
    @pl.when(lax.axis_index("lvl") == 0)
    def _():
        part[...] = near(tall, joined(blocks_of(own, core, core_last)))


def residual_far_kernel(tall, part, cross, rhs, before, resid, mids, skewed):
    big, size = rhs.shape[0] * rhs.shape[1], rhs.shape[1]

    @pl.when(lax.axis_index("lvl") == 0)
    def _():
        value = part[...] + far(tall, joined(blocks_of(cross)))
        store_mids(before[...].reshape(2 * size, -1) - value[big:], mids, skewed)
        resid[...] = rhs[...] - value[:big].reshape(rhs.shape)

    @pl.when(lax.axis_index("lvl") != 0)
    def _():
        resid[...] = jnp.zeros_like(resid)
        mids[...] = jnp.zeros_like(mids)
        skewed[...] = jnp.zeros_like(skewed)


def call(kernel, outs, args, anywhere=0, scratch=(), aliases={}):
    args = [pltpu.with_memory_space_constraint(a, pltpu.HBM) for a in args[:anywhere]] + list(args[anywhere:])
    spaces = [pl.BlockSpec(memory_space=pltpu.HBM)] * anywhere
    spaces += [pl.BlockSpec(memory_space=pltpu.VMEM)] * (len(args) - anywhere)
    return pl.pallas_call(
        kernel,
        out_shape=[jax.ShapeDtypeStruct(shape, dtype) for shape, dtype in outs],
        in_specs=spaces,
        out_specs=[pl.BlockSpec(memory_space=pltpu.VMEM)] * len(outs),
        scratch_shapes=scratch,
        input_output_aliases=aliases,
        compiler_params=pltpu.CompilerParams(vmem_limit_bytes=24 * 1024 * 1024),
        cost_estimate=pl.CostEstimate(flops=0, bytes_accessed=0, transcendentals=0),
    )(*args)


def swaps(rows):
    across = [0] + [r + 1 if r % 2 else r - 1 for r in range(1, rows - 1)] + [rows - 1]
    core = [(l * rows + r, l * rows + (r ^ 1)) for l in range(2) for r in range(rows)]
    cross = [(l * rows + r, l * rows + across[r]) for l in range(2) for r in range(1, rows - 1)]
    cross += [(l * rows + r, (1 - l) * rows + r) for l in range(2) for r in (0, rows - 1)]
    fine = [(r, across[r]) for r in range(1, rows - 1)] + [(0, rows - 1), (rows - 1, 0)]
    fine += [(rows + r, rows + (r ^ 1)) for r in range(rows)]
    short = [(r, across[r]) for r in range(1, rows - 1)] + [(rows + r, rows + (r ^ 1)) for r in range(2, rows - 2)]
    for end, beside in ((0, 1), (rows - 1, rows - 2)):
        short += [(end, rows + end), (rows + end, rows + beside), (rows + beside, end)]
    other = [(r, r ^ 1) for r in range(2, rows - 2)] + [(rows + r, rows + across[r]) for r in range(1, rows - 1)]
    for end, beside in ((0, 1), (rows - 1, rows - 2)):
        other += [(rows + end, end), (end, beside), (beside, rows + end)]
    level = [(l * rows + r, (1 - l) * rows + r) for l in range(2) for r in range(rows)]
    skew = [(r, rows + across[r]) for r in range(1, rows - 1)]
    skew += [(rows + r, r) for r in range(rows) if r not in (1, rows - 2)]
    for end, beside in ((0, 1), (rows - 1, rows - 2)):
        skew += [(end, beside), (rows + beside, rows + end)]
    return tuple((lambda x, pairs=pairs: lax.ppermute(x, ("lvl", "row"), pairs)) for pairs in (core, cross, fine, short, other, level, skew))


def paired(rhs, op_tiles, op_cols, link_tiles, level_links):
    core, cross, fine, short, other, level, skew = swaps(lax.axis_size("row"))
    right, tiles, links = rhs[0, 0], op_tiles[0, 0], link_tiles[0, 0]
    slots, size, width = right.shape
    blocks, pair = (right.shape, F32), ((2, size, width), F32)
    big = slots * size
    codes, goals = jnp.swapaxes(op_cols, 1, 2), jnp.swapaxes(level_links, 2, 3)
    long = ((2 * size + 8, width), F32)
    mids, skewed, payload, wide, restrict = call(
        restrict_kernel,
        [pair, long, blocks, ((2 * size + 8, width), F32), ((4 * size, big), BF16)],
        [goals, right, links],
        anywhere=3,
        scratch=[
            pltpu.SMEM(goals.shape[2:], goals.dtype),
            pltpu.VMEM(links.shape, links.dtype),
            pltpu.SemaphoreType.DMA((3,)),
        ],
    )
    down = result = matrix = prolong = tall = None
    for cycle in range(CYCLES):
        if cycle > 0:
            result_cross = short(result)
            (part,) = call(
                residual_near_kernel,
                [((big + 2 * size, width), F32)],
                [tall, result, core(result[:-1]), core(result[-1:])],
            )
            payload, mids, skewed = call(
                residual_far_kernel,
                [blocks, pair, long],
                [tall, part, result_cross, right, mids],
            )
        mid_here, mid_cross = level(mids), skew(skewed)
        if cycle == 0:
            beyond, beside, mid_core = short(payload), [core(payload)], [core(mid_here)]
            matrix, prolong = call(
                operator_kernel,
                [((2 * big, 3 * big), BF16), ((2 * big, 2 * size), BF16)],
                [codes, goals, links, tiles],
                anywhere=4,
                scratch=[
                    pltpu.SMEM(codes.shape[1:], codes.dtype),
                    pltpu.SMEM(goals.shape[2:], goals.dtype),
                    pltpu.VMEM(links.shape, links.dtype),
                    pltpu.VMEM(tiles.shape, tiles.dtype),
                    pltpu.VMEM((slots, 3 * slots, size, size), F32),
                    pltpu.SemaphoreType.DMA((3 + slots,)),
                ],
            )
            down = payload, beside[0], other(wide)
            part, level_resid = call(
                start_near_kernel,
                [blocks, blocks],
                [matrix, payload, *down[:2], mid_here, *mid_core],
            )
            (first,) = call(
                start_far_kernel,
                [blocks],
                [matrix, part, beyond, down[2], mid_cross],
            )
            (tall,) = call(tall_kernel, [((2 * big + 4 * size, 3 * big), BF16)], [matrix, restrict])
        else:
            beyond, beside = fine(payload), [core(payload[:-1]), core(payload[-1:])]
            mid_core = [core(mid_here[:1]), core(mid_here[1:])]
            (part,) = call(first_fine_kernel, [blocks], [matrix, payload, *beside])
            part, level_resid = call(
                first_near_kernel,
                [blocks, blocks],
                [part, matrix, payload, *down[:2], mid_here, *mid_core],
                aliases={0: 0},
            )
            (first,) = call(first_far_kernel, [blocks], [matrix, part, beyond, down[2], mid_cross])
        first_cross = cross(first)
        (part,) = call(near_kernel, [blocks], [matrix, first, core(first[:-1]), core(first[-1:])])
        smooth, fixes = call(second_kernel, [blocks, pair], [matrix, level_resid, first, part, first_cross, prolong])
        fixes = level(fixes)
        args = [smooth, fixes, prolong] + ([] if cycle == 0 else [result])
        (result,) = call(solution_kernel, [blocks], args)
    return result[None, None]


def body(rhs, *rest):
    rows = lax.axis_size("row")
    square = rhs.shape[-1] == rhs.shape[-2]
    plan = paired if lax.axis_size("lvl") == 2 and rows % 2 == 0 and rows > 2 and square else per_device
    return plan(rhs, *rest)


def solution(mesh):
    placed = (
        P("lvl", "row", None, None, None),
        P("lvl", "row", None, None, None, None),
        P("lvl", "row", None, None),
        P("lvl", "row", None, None, None, None),
        P("lvl", "row", None, None),
    )
    return jax.shard_map(
        body,
        mesh=mesh,
        in_specs=placed,
        out_specs=P("lvl", "row", None, None, None),
        check_vma=False,
    )
```

```python
import functools

import jax
import jax.numpy as jnp
from jax import lax
from jax.experimental import pallas as pl
from jax.experimental.pallas import tpu as pltpu
from jax.sharding import PartitionSpec as P

CYCLES = 2


HIGH = lax.Precision.HIGHEST
COEF_ZERO = 0.9
COEF_ONE = -0.36
COEF_TWO = 0.05
F32 = jnp.float32
BF16 = jnp.bfloat16


def extended(block, sides, width):
    for axis, dim in sides:
        count = lax.axis_size(axis)
        forward = [(i, i + 1) for i in range(count - 1)]
        backward = [(target, source) for source, target in forward]
        low = lax.ppermute(
            lax.slice_in_dim(block, block.shape[dim] - width, None, axis=dim), axis, forward
        )
        high = lax.ppermute(lax.slice_in_dim(block, 0, width, axis=dim), axis, backward)
        block = jnp.concatenate([low, block, high], axis=dim)
    return block


def broadcast(block, axis, source):
    block = jnp.where(lax.axis_index(axis) == source, block, jnp.zeros_like(block))
    return lax.psum(block, axis)


def apply_operator(field, tiles, columns, keep):
    slots = field.shape[0]
    padded = extended(field[None], (("row", 0),), 1)
    candidates = padded.reshape((3 * slots,) + field.shape[1:])
    picked = candidates[columns]
    image = jnp.einsum("sjab,sjbn->san", tiles, picked, precision=HIGH)
    return image * keep[:, None, None]


def per_device(rhs, op_tiles, op_cols, link_tiles, level_links):
    n_lvl = lax.axis_size("lvl")
    fine_lvls = 5 * n_lvl // 8
    mid_lvls = max(n_lvl - fine_lvls - 1, 1)
    lvl_here = lax.axis_index("lvl")
    right = rhs[0, 0]
    tiles = op_tiles[0, 0]
    columns = op_cols[0, 0]
    links = link_tiles[0, 0]
    targets = level_links[0, 0]
    slots = right.shape[0]
    slot_ids = jnp.arange(slots)
    pair_ids = jnp.arange(2)
    is_fine = lvl_here < fine_lvls
    is_mid = (lvl_here >= fine_lvls) & (lvl_here < fine_lvls + mid_lvls)
    is_coarse = lvl_here == n_lvl - 1
    fine_keep = jnp.where(is_fine & (slot_ids >= 0), 1.0, 0.0).astype(jnp.float32)
    mid_keep = jnp.where(is_mid & ((slot_ids == 0) | (slot_ids == 2)), 1.0, 0.0).astype(jnp.float32)
    coarse_keep = jnp.where(is_coarse & (slot_ids == 1), 1.0, 0.0).astype(jnp.float32)
    all_keep = fine_keep + mid_keep + coarse_keep
    mid_flag = jnp.where(is_mid, 1.0, 0.0).astype(jnp.float32)
    place = (slot_ids[:, None] == 2 * pair_ids[None, :]).astype(jnp.float32) * mid_flag
    lvl_ids = jnp.arange(n_lvl)

    def lvl_table(target):
        by_lvl = (target[:, None] // 2 + fine_lvls == lvl_ids[None, :]).astype(jnp.float32)
        by_pair = (target[:, None] % 2 == pair_ids[None, :]).astype(jnp.float32)
        return by_lvl[:, :, None] * by_pair[:, None, :] * fine_keep[:, None, None]

    to_lvl = lvl_table(targets[:, 0])
    from_lvl = lvl_table(targets[:, 1])
    mid_restrict = jnp.stack([links[0, 0], links[2, 0]])
    mid_prolong = jnp.stack([links[0, 1], links[2, 1]])
    solution = jnp.zeros_like(right)
    mid_fix = jnp.zeros((2,) + right.shape[1:], jnp.float32)
    coarse_fix = jnp.zeros_like(right[0])
    for cycle in range(CYCLES):
        if cycle == 0:
            resid = right * fine_keep[:, None, None]
        else:
            resid = (right - apply_operator(solution, tiles, columns, all_keep)) * fine_keep[
                :, None, None
            ]
        terms = jnp.einsum("sab,sbn->san", links[:, 0], resid, precision=HIGH)
        dense = jnp.einsum("slm,san->lman", to_lvl, terms, precision=HIGH)
        mid_resid = lax.psum_scatter(dense, "lvl", scatter_dimension=0, tiled=True)[0] * mid_flag
        mid_part = jnp.einsum("mab,mbn->an", mid_restrict, mid_resid, precision=HIGH) * mid_flag
        fine_part = 0.5 * jnp.sum(terms * fine_keep[:, None, None], axis=0)
        coarse_resid = lax.psum(mid_part + fine_part, "lvl")
        level_resid = resid + jnp.einsum("sm,man->san", place, mid_resid, precision=HIGH)
        level_resid = level_resid + coarse_keep[:, None, None] * coarse_resid[None]
        first = apply_operator(level_resid, tiles, columns, all_keep)
        second = apply_operator(first, tiles, columns, all_keep)
        smooth = COEF_ZERO * level_resid + COEF_ONE * first + COEF_TWO * second
        coarse_fix = broadcast(smooth[1], "lvl", n_lvl - 1)
        mid_fix = jnp.stack([smooth[0], smooth[2]]) + jnp.einsum(
            "mab,bn->man", mid_prolong, coarse_fix, precision=HIGH
        )
        gathered = lax.all_gather(mid_fix[None], "lvl", axis=0, tiled=True)
        chosen = jnp.einsum("slm,lman->san", from_lvl, gathered, precision=HIGH)
        chosen = chosen + coarse_fix[None]
        fine_fix = smooth + jnp.einsum("sab,sbn->san", links[:, 1], chosen, precision=HIGH)
        solution = solution + fine_fix * fine_keep[:, None, None]
    levels = solution * fine_keep[:, None, None] + jnp.einsum(
        "sm,man->san", place, mid_fix, precision=HIGH
    )
    levels = levels + coarse_keep[:, None, None] * coarse_fix[None]
    return levels[None, None]


def split(value):
    high = value.astype(BF16)
    return high, (value - high.astype(F32)).astype(BF16)


def split_rows(value):
    return jnp.concatenate(split(value), axis=0)


def split_columns(value):
    return jnp.concatenate(split(value), axis=1)


def product(left, right):
    full = jnp.dot(left, right, preferred_element_type=F32)
    rows, columns = full.shape[0] // 2, full.shape[1] // 2
    small = full[rows:, :columns] + full[:rows, columns:] + full[rows:, columns:]
    return full[:rows, :columns] + small


def stacked(*blocks):
    return jnp.concatenate(blocks, axis=0)


def store_mids(value, mids, skewed):
    mids[...] = value.reshape(mids.shape)
    skewed[:value.shape[0], :] = value
    skewed[value.shape[0]:, :] = jnp.zeros_like(skewed[value.shape[0]:, :])


def restrict_kernel(targets_in, rhs_in, links_in, mids, skewed, payload, wide, restrict, targets, links, sems):
    size = payload.shape[-1]
    slots = payload.shape[0]
    fetch_targets = pltpu.make_async_copy(targets_in.at[0, 0], targets, sems.at[0])
    fetch_links = pltpu.make_async_copy(links_in, links, sems.at[1])
    fetch_rhs = pltpu.make_async_copy(rhs_in, payload, sems.at[2])
    fetch_targets.start()
    fetch_links.start()

    @pl.when(lax.axis_index("lvl") == 0)
    def _():
        fetch_rhs.start()
        fetch_targets.wait()
        fetch_links.wait()
        for s in range(slots):
            for k in range(2):
                down = jnp.where(targets[0, s] == k, links[s, 0], 0.0)
                high, low = split(down)
                restrict[k * size:(k + 1) * size, s * size:(s + 1) * size] = high
                restrict[(2 + k) * size:(3 + k) * size, s * size:(s + 1) * size] = low
        fetch_rhs.wait()
        right = split_columns(payload[...].reshape(slots * size, size))
        store_mids(product(restrict[...], right), mids, skewed)
        wide[...] = jnp.zeros_like(wide)

    @pl.when(lax.axis_index("lvl") != 0)
    def _():
        fetch_targets.wait()
        fetch_links.wait()
        payload[0] = links[0, 0]
        payload[1] = links[2, 0]
        payload[2] = jnp.zeros_like(payload[2])
        wide[:2 * size, :] = stacked(links[0, 0], links[2, 0])
        wide[2 * size:, :] = jnp.zeros_like(wide[2 * size:, :])
        mids[...] = jnp.zeros_like(mids)
        skewed[...] = jnp.zeros_like(skewed)


def operator_kernel(columns_in, targets_in, links_in, tiles_in, matrix, prolong, columns, targets, links, tiles, gathered, sems):
    slots, count, size = tiles.shape[0], tiles.shape[1], tiles.shape[-1]
    fetch_columns = pltpu.make_async_copy(columns_in.at[0], columns, sems.at[0])
    fetch_targets = pltpu.make_async_copy(targets_in.at[0, 0], targets, sems.at[1])
    fetch_links = pltpu.make_async_copy(links_in, links, sems.at[2])
    fetch_tiles = [pltpu.make_async_copy(tiles_in.at[s], tiles.at[s], sems.at[3 + s]) for s in range(slots)]
    for fetch in (fetch_columns, fetch_targets, *fetch_tiles, fetch_links):
        fetch.start()
    row = lax.axis_index("row")
    odd = lax.rem(row, 2)
    inner = (row > 0) & (row < lax.axis_size("row") - 1)
    gathered[...] = jnp.zeros_like(gathered)
    fetch_columns.wait()
    fetch_targets.wait()
    for s in range(slots):
        fetch_tiles[s].wait()
        for j in range(count):
            code = columns[s, 0, j]
            step = code // slots
            slot = code - slots * step
            side = jnp.where(step == 1, 0, jnp.where(step == 2 * (1 - odd), 1, 2))
            gathered[s, side * slots + slot] += tiles[s, j]
        for c in range(3 * slots):
            block = gathered[s, c]
            if c >= 2 * slots:
                block = jnp.where(inner, block, 0.0)
            high, low = split(block)
            matrix[s * size:(s + 1) * size, c * size:(c + 1) * size] = high
            matrix[(slots + s) * size:(slots + s + 1) * size, c * size:(c + 1) * size] = low
    fetch_links.wait()

    @pl.when(lax.axis_index("lvl") == 0)
    def _():
        for s in range(slots):
            for k in range(2):
                up = jnp.where(targets[1, s] == k, links[s, 1], 0.0)
                high, low = split(up)
                prolong[s * size:(s + 1) * size, k * size:(k + 1) * size] = high
                prolong[(slots + s) * size:(slots + s + 1) * size, k * size:(k + 1) * size] = low

    @pl.when(lax.axis_index("lvl") != 0)
    def _():
        prolong[:4 * size, :size] = split_rows(stacked(links[0, 1], links[2, 1]))


def joined(blocks):
    return split_columns(stacked(*blocks))


def blocks_of(*refs):
    return [ref[s] for ref in refs for s in range(ref.shape[0])]


def own_slots(matrix, sides, groups):
    size = groups[0][0].shape[0]
    slots = len(groups[0])
    parts = []
    for s in range(slots):
        columns = [slice((side * slots + s) * size, (side * slots + s + 1) * size) for side in sides]
        high = [matrix[s * size:(s + 1) * size, c] for c in columns]
        low = [matrix[(slots + s) * size:(slots + s + 1) * size, c] for c in columns]
        left = stacked(jnp.concatenate(high, axis=1), jnp.concatenate(low, axis=1))
        parts.append(product(left, joined([group[s] for group in groups])))
    return stacked(*parts).reshape(slots, size, -1)


def near(matrix, field):
    columns = 2 * (matrix.shape[1] // 3)
    return product(matrix[:, :columns], field)


def far(matrix, field):
    columns = 2 * (matrix.shape[1] // 3)
    return product(matrix[:, columns:], field)


def level_blocks(down, mid):
    left = split_rows(jnp.concatenate([down[0], down[1]], axis=1))
    coarse = product(left, joined((mid[0], mid[1]))) + 0.5 * (mid[0] + mid[1])
    return [mid[0], coarse, mid[1]]


def rows_of(ref):
    size = ref.shape[-1]
    return [ref[k * size:(k + 1) * size, :] for k in range(2)]


def first_fine_kernel(matrix, own, *rest):
    *core, part = rest

    @pl.when(lax.axis_index("lvl") == 0)
    def _():
        part[...] = near(matrix, joined(blocks_of(own, *core))).reshape(part.shape)


def first_near_kernel(fine_part, matrix, own, down_own, down_core, mid_own, mid_core, mid_core_last, part, level):
    @pl.when(lax.axis_index("lvl") == 0)
    def _():
        level[...] = own[...]

    @pl.when(lax.axis_index("lvl") != 0)
    def _():
        here = level_blocks(down_own, blocks_of(mid_own))
        beside = level_blocks(down_core, blocks_of(mid_core, mid_core_last))
        level[...] = stacked(*here).reshape(level.shape)
        part[...] = own_slots(matrix, (0, 1), (here, beside))


def start_near_kernel(matrix, own, down_own, down_core, mid_own, mid_core, part, level):
    @pl.when(lax.axis_index("lvl") == 0)
    def _():
        level[...] = own[...]
        part[...] = near(matrix, joined(blocks_of(own, down_core))).reshape(part.shape)

    @pl.when(lax.axis_index("lvl") != 0)
    def _():
        here = level_blocks(down_own, blocks_of(mid_own))
        beside = level_blocks(down_core, blocks_of(mid_core))
        level[...] = stacked(*here).reshape(level.shape)
        part[...] = own_slots(matrix, (0, 1), (here, beside))


def start_far_kernel(matrix, part, cross, down_cross, skewed, first):
    @pl.when(lax.axis_index("lvl") == 0)
    def _():
        first[...] = part[...] + far(matrix, joined(blocks_of(cross))).reshape(first.shape)

    @pl.when(lax.axis_index("lvl") != 0)
    def _():
        beside = level_blocks(rows_of(down_cross), rows_of(skewed))
        first[...] = part[...] + own_slots(matrix, (2,), (beside,))


def first_far_kernel(matrix, part, cross, down_cross, skewed, first):
    @pl.when(lax.axis_index("lvl") == 0)
    def _():
        first[...] = part[...] + far(matrix, joined(blocks_of(cross))).reshape(first.shape)

    @pl.when(lax.axis_index("lvl") != 0)
    def _():
        beside = level_blocks(rows_of(down_cross), rows_of(skewed))
        first[...] = part[...] + own_slots(matrix, (2,), (beside,))


def near_kernel(matrix, own, core, core_last, part):
    @pl.when(lax.axis_index("lvl") == 0)
    def _():
        part[...] = near(matrix, joined(blocks_of(own, core, core_last))).reshape(part.shape)

    @pl.when(lax.axis_index("lvl") != 0)
    def _():
        part[...] = own_slots(matrix, (0, 1), (blocks_of(own), blocks_of(core, core_last)))


def fix_kernel(matrix, level, own, part, cross, prolong, smooth, fixes):
    @pl.when(lax.axis_index("lvl") == 0)
    def _():
        fixes[...] = jnp.zeros_like(fixes)

    @pl.when(lax.axis_index("lvl") != 0)
    def _():
        second = part[...] + own_slots(matrix, (2,), (blocks_of(cross),))
        value = COEF_ZERO * level[...] + COEF_ONE * own[...] + COEF_TWO * second
        coarse = value[1]
        size = coarse.shape[0]
        up = product(prolong[:4 * size, :size], split_columns(coarse))
        low, high = value[0] + up[:size], value[2] + up[size:]
        fixes[0] = low + coarse
        fixes[1] = high + coarse
        smooth[0] = low
        smooth[1] = coarse
        smooth[2] = high


def smooth_kernel(passed, matrix, level, own, part, cross, *rest):
    smooth = rest[-1]

    @pl.when(lax.axis_index("lvl") == 0)
    def _():
        second = part[...] + far(matrix, joined(blocks_of(cross))).reshape(part.shape)
        value = COEF_ZERO * level[...] + COEF_ONE * own[...] + COEF_TWO * second
        smooth[...] = value if len(rest) == 1 else rest[0][...] + value


def solution_kernel(smooth, fixes, prolong, result):
    @pl.when(lax.axis_index("lvl") == 0)
    def _():
        result[...] = smooth[...] + product(prolong[...], joined(blocks_of(fixes))).reshape(smooth.shape)

    @pl.when(lax.axis_index("lvl") != 0)
    def _():
        result[...] = smooth[...]


def tall_kernel(matrix, restrict, tall):
    big, wide = matrix.shape[0] // 2, restrict.shape[0] // 2

    @pl.when(lax.axis_index("lvl") == 0)
    def _():
        tall[:big, :] = matrix[:big, :]
        tall[big + wide:2 * big + wide, :] = matrix[big:, :]
        for c in range(0, matrix.shape[1], big):
            right = jnp.concatenate([matrix[:big, c:c + big], matrix[big:, c:c + big]], axis=1)
            high, low = split(product(restrict[...], right))
            tall[big:big + wide, c:c + big] = high
            tall[2 * big + wide:, c:c + big] = low


def residual_near_kernel(tall, own, core, core_last, part):
    @pl.when(lax.axis_index("lvl") == 0)
    def _():
        part[...] = near(tall, joined(blocks_of(own, core, core_last)))


def residual_far_kernel(tall, part, cross, rhs, before, resid, mids, skewed):
    big, size = rhs.shape[0] * rhs.shape[1], rhs.shape[1]

    @pl.when(lax.axis_index("lvl") == 0)
    def _():
        value = part[...] + far(tall, joined(blocks_of(cross)))
        store_mids(before[...].reshape(2 * size, -1) - value[big:], mids, skewed)
        resid[...] = rhs[...] - value[:big].reshape(rhs.shape)

    @pl.when(lax.axis_index("lvl") != 0)
    def _():
        resid[...] = jnp.zeros_like(resid)
        mids[...] = jnp.zeros_like(mids)
        skewed[...] = jnp.zeros_like(skewed)


def call(kernel, outs, args, anywhere=0, scratch=(), aliases={}):
    args = [pltpu.with_memory_space_constraint(a, pltpu.HBM) for a in args[:anywhere]] + list(args[anywhere:])
    spaces = [pl.BlockSpec(memory_space=pltpu.HBM)] * anywhere
    spaces += [pl.BlockSpec(memory_space=pltpu.VMEM)] * (len(args) - anywhere)
    return pl.pallas_call(
        kernel,
        out_shape=[jax.ShapeDtypeStruct(shape, dtype) for shape, dtype in outs],
        in_specs=spaces,
        out_specs=[pl.BlockSpec(memory_space=pltpu.VMEM)] * len(outs),
        scratch_shapes=scratch,
        input_output_aliases=aliases,
        compiler_params=pltpu.CompilerParams(vmem_limit_bytes=24 * 1024 * 1024),
        cost_estimate=pl.CostEstimate(flops=0, bytes_accessed=0, transcendentals=0),
    )(*args)


def swaps(rows):
    across = [0] + [r + 1 if r % 2 else r - 1 for r in range(1, rows - 1)] + [rows - 1]
    core = [(l * rows + r, l * rows + (r ^ 1)) for l in range(2) for r in range(rows)]
    cross = [(l * rows + r, l * rows + across[r]) for l in range(2) for r in range(1, rows - 1)]
    cross += [(l * rows + r, (1 - l) * rows + r) for l in range(2) for r in (0, rows - 1)]
    fine = [(r, across[r]) for r in range(1, rows - 1)] + [(0, rows - 1), (rows - 1, 0)]
    fine += [(rows + r, rows + (r ^ 1)) for r in range(rows)]
    short = [(r, across[r]) for r in range(1, rows - 1)] + [(rows + r, rows + (r ^ 1)) for r in range(2, rows - 2)]
    for end, beside in ((0, 1), (rows - 1, rows - 2)):
        short += [(end, rows + beside), (rows + beside, rows + end), (rows + end, end)]
    other = [(r, r ^ 1) for r in range(2, rows - 2)] + [(rows + r, rows + across[r]) for r in range(1, rows - 1)]
    for end, beside in ((0, 1), (rows - 1, rows - 2)):
        other += [(rows + end, end), (end, beside), (beside, rows + end)]
    level = [(l * rows + r, (1 - l) * rows + r) for l in range(2) for r in range(rows)]
    skew = [(r, rows + across[r]) for r in range(1, rows - 1)]
    skew += [(rows + r, r) for r in range(rows) if r not in (1, rows - 2)]
    for end, beside in ((0, 1), (rows - 1, rows - 2)):
        skew += [(end, beside), (rows + beside, rows + end)]
    return tuple((lambda x, pairs=pairs: lax.ppermute(x, ("lvl", "row"), pairs)) for pairs in (core, cross, fine, short, other, level, skew))


def paired(rhs, op_tiles, op_cols, link_tiles, level_links):
    core, cross, fine, short, other, level, skew = swaps(lax.axis_size("row"))
    right, tiles, links = rhs[0, 0], op_tiles[0, 0], link_tiles[0, 0]
    slots, size, width = right.shape
    blocks, pair = (right.shape, F32), ((2, size, width), F32)
    big = slots * size
    codes, goals = jnp.swapaxes(op_cols, 1, 2), jnp.swapaxes(level_links, 2, 3)
    long = ((2 * size + 8, width), F32)
    mids, skewed, payload, wide, restrict = call(
        restrict_kernel,
        [pair, long, blocks, ((2 * size + 8, width), F32), ((4 * size, big), BF16)],
        [goals, right, links],
        anywhere=3,
        scratch=[
            pltpu.SMEM(goals.shape[2:], goals.dtype),
            pltpu.VMEM(links.shape, links.dtype),
            pltpu.SemaphoreType.DMA((3,)),
        ],
    )
    down = result = matrix = prolong = tall = None
    for cycle in range(CYCLES):
        if cycle > 0:
            result_cross = short(result)
            (part,) = call(
                residual_near_kernel,
                [((big + 2 * size, width), F32)],
                [tall, result, core(result[:-1]), core(result[-1:])],
            )
            payload, mids, skewed = call(
                residual_far_kernel,
                [blocks, pair, long],
                [tall, part, result_cross, right, mids],
            )
        mid_here, mid_cross = level(mids), skew(skewed)
        if cycle == 0:
            beyond, beside, mid_core = short(payload), [core(payload)], [core(mid_here)]
            matrix, prolong = call(
                operator_kernel,
                [((2 * big, 3 * big), BF16), ((2 * big, 2 * size), BF16)],
                [codes, goals, links, tiles],
                anywhere=4,
                scratch=[
                    pltpu.SMEM(codes.shape[1:], codes.dtype),
                    pltpu.SMEM(goals.shape[2:], goals.dtype),
                    pltpu.VMEM(links.shape, links.dtype),
                    pltpu.VMEM(tiles.shape, tiles.dtype),
                    pltpu.VMEM((slots, 3 * slots, size, size), F32),
                    pltpu.SemaphoreType.DMA((3 + slots,)),
                ],
            )
            down = payload, beside[0], other(wide)
            part, level_resid = call(
                start_near_kernel,
                [blocks, blocks],
                [matrix, payload, *down[:2], mid_here, *mid_core],
            )
            (first,) = call(
                start_far_kernel,
                [blocks],
                [matrix, part, beyond, down[2], mid_cross],
            )
            (tall,) = call(tall_kernel, [((2 * big + 4 * size, 3 * big), BF16)], [matrix, restrict])
        else:
            beyond, beside = fine(payload), [core(payload)]
            mid_core = [core(mid_here[:1]), core(mid_here[1:])]
            (part,) = call(first_fine_kernel, [blocks], [matrix, payload, *beside])
            part, level_resid = call(
                first_near_kernel,
                [blocks, blocks],
                [part, matrix, payload, *down[:2], mid_here, *mid_core],
                aliases={0: 0},
            )
            (first,) = call(first_far_kernel, [blocks], [matrix, part, beyond, down[2], mid_cross])
        first_cross = cross(first)
        (part,) = call(near_kernel, [blocks], [matrix, first, core(first[:-1]), core(first[-1:])])
        known = [matrix, level_resid, first, part, first_cross]
        smooth, fixes = call(fix_kernel, [blocks, pair], [*known, prolong])
        fixes = level(fixes)
        before = [] if cycle == 0 else [result]
        (smooth,) = call(smooth_kernel, [blocks], [smooth, *known, *before], aliases={0: 0})
        (result,) = call(solution_kernel, [blocks], [smooth, fixes, prolong])
    return result[None, None]


def body(rhs, *rest):
    rows = lax.axis_size("row")
    square = rhs.shape[-1] == rhs.shape[-2]
    plan = paired if lax.axis_size("lvl") == 2 and rows % 2 == 0 and rows > 2 and square else per_device
    return plan(rhs, *rest)


def solution(mesh):
    placed = (
        P("lvl", "row", None, None, None),
        P("lvl", "row", None, None, None, None),
        P("lvl", "row", None, None),
        P("lvl", "row", None, None, None, None),
        P("lvl", "row", None, None),
    )
    return jax.shard_map(
        body,
        mesh=mesh,
        in_specs=placed,
        out_specs=P("lvl", "row", None, None, None),
        check_vma=False,
    )
```

```python
import functools

import jax
import jax.numpy as jnp
from jax import lax
from jax.experimental import pallas as pl
from jax.experimental.pallas import tpu as pltpu
from jax.sharding import PartitionSpec as P

CYCLES = 2


HIGH = lax.Precision.HIGHEST
COEF_ZERO = 0.9
COEF_ONE = -0.36
COEF_TWO = 0.05
F32 = jnp.float32
BF16 = jnp.bfloat16


def extended(block, sides, width):
    for axis, dim in sides:
        count = lax.axis_size(axis)
        forward = [(i, i + 1) for i in range(count - 1)]
        backward = [(target, source) for source, target in forward]
        low = lax.ppermute(
            lax.slice_in_dim(block, block.shape[dim] - width, None, axis=dim), axis, forward
        )
        high = lax.ppermute(lax.slice_in_dim(block, 0, width, axis=dim), axis, backward)
        block = jnp.concatenate([low, block, high], axis=dim)
    return block


def broadcast(block, axis, source):
    block = jnp.where(lax.axis_index(axis) == source, block, jnp.zeros_like(block))
    return lax.psum(block, axis)


def apply_operator(field, tiles, columns, keep):
    slots = field.shape[0]
    padded = extended(field[None], (("row", 0),), 1)
    candidates = padded.reshape((3 * slots,) + field.shape[1:])
    picked = candidates[columns]
    image = jnp.einsum("sjab,sjbn->san", tiles, picked, precision=HIGH)
    return image * keep[:, None, None]


def per_device(rhs, op_tiles, op_cols, link_tiles, level_links):
    n_lvl = lax.axis_size("lvl")
    fine_lvls = 5 * n_lvl // 8
    mid_lvls = max(n_lvl - fine_lvls - 1, 1)
    lvl_here = lax.axis_index("lvl")
    right = rhs[0, 0]
    tiles = op_tiles[0, 0]
    columns = op_cols[0, 0]
    links = link_tiles[0, 0]
    targets = level_links[0, 0]
    slots = right.shape[0]
    slot_ids = jnp.arange(slots)
    pair_ids = jnp.arange(2)
    is_fine = lvl_here < fine_lvls
    is_mid = (lvl_here >= fine_lvls) & (lvl_here < fine_lvls + mid_lvls)
    is_coarse = lvl_here == n_lvl - 1
    fine_keep = jnp.where(is_fine & (slot_ids >= 0), 1.0, 0.0).astype(jnp.float32)
    mid_keep = jnp.where(is_mid & ((slot_ids == 0) | (slot_ids == 2)), 1.0, 0.0).astype(jnp.float32)
    coarse_keep = jnp.where(is_coarse & (slot_ids == 1), 1.0, 0.0).astype(jnp.float32)
    all_keep = fine_keep + mid_keep + coarse_keep
    mid_flag = jnp.where(is_mid, 1.0, 0.0).astype(jnp.float32)
    place = (slot_ids[:, None] == 2 * pair_ids[None, :]).astype(jnp.float32) * mid_flag
    lvl_ids = jnp.arange(n_lvl)

    def lvl_table(target):
        by_lvl = (target[:, None] // 2 + fine_lvls == lvl_ids[None, :]).astype(jnp.float32)
        by_pair = (target[:, None] % 2 == pair_ids[None, :]).astype(jnp.float32)
        return by_lvl[:, :, None] * by_pair[:, None, :] * fine_keep[:, None, None]

    to_lvl = lvl_table(targets[:, 0])
    from_lvl = lvl_table(targets[:, 1])
    mid_restrict = jnp.stack([links[0, 0], links[2, 0]])
    mid_prolong = jnp.stack([links[0, 1], links[2, 1]])
    solution = jnp.zeros_like(right)
    mid_fix = jnp.zeros((2,) + right.shape[1:], jnp.float32)
    coarse_fix = jnp.zeros_like(right[0])
    for cycle in range(CYCLES):
        if cycle == 0:
            resid = right * fine_keep[:, None, None]
        else:
            resid = (right - apply_operator(solution, tiles, columns, all_keep)) * fine_keep[
                :, None, None
            ]
        terms = jnp.einsum("sab,sbn->san", links[:, 0], resid, precision=HIGH)
        dense = jnp.einsum("slm,san->lman", to_lvl, terms, precision=HIGH)
        mid_resid = lax.psum_scatter(dense, "lvl", scatter_dimension=0, tiled=True)[0] * mid_flag
        mid_part = jnp.einsum("mab,mbn->an", mid_restrict, mid_resid, precision=HIGH) * mid_flag
        fine_part = 0.5 * jnp.sum(terms * fine_keep[:, None, None], axis=0)
        coarse_resid = lax.psum(mid_part + fine_part, "lvl")
        level_resid = resid + jnp.einsum("sm,man->san", place, mid_resid, precision=HIGH)
        level_resid = level_resid + coarse_keep[:, None, None] * coarse_resid[None]
        first = apply_operator(level_resid, tiles, columns, all_keep)
        second = apply_operator(first, tiles, columns, all_keep)
        smooth = COEF_ZERO * level_resid + COEF_ONE * first + COEF_TWO * second
        coarse_fix = broadcast(smooth[1], "lvl", n_lvl - 1)
        mid_fix = jnp.stack([smooth[0], smooth[2]]) + jnp.einsum(
            "mab,bn->man", mid_prolong, coarse_fix, precision=HIGH
        )
        gathered = lax.all_gather(mid_fix[None], "lvl", axis=0, tiled=True)
        chosen = jnp.einsum("slm,lman->san", from_lvl, gathered, precision=HIGH)
        chosen = chosen + coarse_fix[None]
        fine_fix = smooth + jnp.einsum("sab,sbn->san", links[:, 1], chosen, precision=HIGH)
        solution = solution + fine_fix * fine_keep[:, None, None]
    levels = solution * fine_keep[:, None, None] + jnp.einsum(
        "sm,man->san", place, mid_fix, precision=HIGH
    )
    levels = levels + coarse_keep[:, None, None] * coarse_fix[None]
    return levels[None, None]


def split(value):
    high = value.astype(BF16)
    return high, (value - high.astype(F32)).astype(BF16)


def split_rows(value):
    return jnp.concatenate(split(value), axis=0)


def split_columns(value):
    return jnp.concatenate(split(value), axis=1)


def product(left, right):
    full = jnp.dot(left, right, preferred_element_type=F32)
    rows, columns = full.shape[0] // 2, full.shape[1] // 2
    small = full[rows:, :columns] + full[:rows, columns:] + full[rows:, columns:]
    return full[:rows, :columns] + small


def stacked(*blocks):
    return jnp.concatenate(blocks, axis=0)


def store_mids(value, mids, skewed):
    mids[...] = value.reshape(mids.shape)
    skewed[:value.shape[0], :] = value
    skewed[value.shape[0]:, :] = jnp.zeros_like(skewed[value.shape[0]:, :])


def restrict_kernel(targets_in, rhs_in, links_in, mids, skewed, payload, wide, restrict, targets, links, sems):
    size = payload.shape[-1]
    slots = payload.shape[0]
    fetch_targets = pltpu.make_async_copy(targets_in.at[0, 0], targets, sems.at[0])
    fetch_links = pltpu.make_async_copy(links_in, links, sems.at[1])
    fetch_rhs = pltpu.make_async_copy(rhs_in, payload, sems.at[2])
    fetch_targets.start()
    fetch_links.start()

    @pl.when(lax.axis_index("lvl") == 0)
    def _():
        fetch_rhs.start()
        fetch_targets.wait()
        fetch_links.wait()
        for s in range(slots):
            for k in range(2):
                down = jnp.where(targets[0, s] == k, links[s, 0], 0.0)
                high, low = split(down)
                restrict[k * size:(k + 1) * size, s * size:(s + 1) * size] = high
                restrict[(2 + k) * size:(3 + k) * size, s * size:(s + 1) * size] = low
        fetch_rhs.wait()
        right = split_columns(payload[...].reshape(slots * size, size))
        store_mids(product(restrict[...], right), mids, skewed)
        wide[...] = jnp.zeros_like(wide)

    @pl.when(lax.axis_index("lvl") != 0)
    def _():
        fetch_targets.wait()
        fetch_links.wait()
        payload[0] = links[0, 0]
        payload[1] = links[2, 0]
        payload[2] = jnp.zeros_like(payload[2])
        wide[:2 * size, :] = stacked(links[0, 0], links[2, 0])
        wide[2 * size:, :] = jnp.zeros_like(wide[2 * size:, :])
        mids[...] = jnp.zeros_like(mids)
        skewed[...] = jnp.zeros_like(skewed)


def operator_kernel(columns_in, targets_in, links_in, tiles_in, matrix, prolong, columns, targets, links, tiles, gathered, sems):
    slots, count, size = tiles.shape[0], tiles.shape[1], tiles.shape[-1]
    fetch_columns = pltpu.make_async_copy(columns_in.at[0], columns, sems.at[0])
    fetch_targets = pltpu.make_async_copy(targets_in.at[0, 0], targets, sems.at[1])
    fetch_links = pltpu.make_async_copy(links_in, links, sems.at[2])
    fetch_tiles = [pltpu.make_async_copy(tiles_in.at[s], tiles.at[s], sems.at[3 + s]) for s in range(slots)]
    for fetch in (fetch_columns, fetch_targets, *fetch_tiles, fetch_links):
        fetch.start()
    row = lax.axis_index("row")
    odd = lax.rem(row, 2)
    inner = (row > 0) & (row < lax.axis_size("row") - 1)
    gathered[...] = jnp.zeros_like(gathered)
    fetch_columns.wait()
    fetch_targets.wait()
    for s in range(slots):
        fetch_tiles[s].wait()
        for j in range(count):
            code = columns[s, 0, j]
            step = code // slots
            slot = code - slots * step
            side = jnp.where(step == 1, 0, jnp.where(step == 2 * (1 - odd), 1, 2))
            gathered[s, side * slots + slot] += tiles[s, j]
        for c in range(3 * slots):
            block = gathered[s, c]
            if c >= 2 * slots:
                block = jnp.where(inner, block, 0.0)
            high, low = split(block)
            matrix[s * size:(s + 1) * size, c * size:(c + 1) * size] = high
            matrix[(slots + s) * size:(slots + s + 1) * size, c * size:(c + 1) * size] = low
    fetch_links.wait()

    @pl.when(lax.axis_index("lvl") == 0)
    def _():
        for s in range(slots):
            for k in range(2):
                up = jnp.where(targets[1, s] == k, links[s, 1], 0.0)
                high, low = split(up)
                prolong[s * size:(s + 1) * size, k * size:(k + 1) * size] = high
                prolong[(slots + s) * size:(slots + s + 1) * size, k * size:(k + 1) * size] = low

    @pl.when(lax.axis_index("lvl") != 0)
    def _():
        prolong[:4 * size, :size] = split_rows(stacked(links[0, 1], links[2, 1]))


def joined(blocks):
    return split_columns(stacked(*blocks))


def blocks_of(*refs):
    return [ref[s] for ref in refs for s in range(ref.shape[0])]


def own_slots(matrix, sides, groups):
    size = groups[0][0].shape[0]
    slots = len(groups[0])
    parts = []
    for s in range(slots):
        columns = [slice((side * slots + s) * size, (side * slots + s + 1) * size) for side in sides]
        high = [matrix[s * size:(s + 1) * size, c] for c in columns]
        low = [matrix[(slots + s) * size:(slots + s + 1) * size, c] for c in columns]
        left = stacked(jnp.concatenate(high, axis=1), jnp.concatenate(low, axis=1))
        parts.append(product(left, joined([group[s] for group in groups])))
    return stacked(*parts).reshape(slots, size, -1)


def near(matrix, field):
    columns = 2 * (matrix.shape[1] // 3)
    return product(matrix[:, :columns], field)


def far(matrix, field):
    columns = 2 * (matrix.shape[1] // 3)
    return product(matrix[:, columns:], field)


def level_blocks(down, mid):
    left = split_rows(jnp.concatenate([down[0], down[1]], axis=1))
    coarse = product(left, joined((mid[0], mid[1]))) + 0.5 * (mid[0] + mid[1])
    return [mid[0], coarse, mid[1]]


def rows_of(ref):
    size = ref.shape[-1]
    return [ref[k * size:(k + 1) * size, :] for k in range(2)]


def first_fine_kernel(matrix, own, *rest):
    *core, part = rest

    @pl.when(lax.axis_index("lvl") == 0)
    def _():
        part[...] = near(matrix, joined(blocks_of(own, *core))).reshape(part.shape)


def first_near_kernel(fine_part, matrix, own, down_own, down_core, mid_own, mid_core, mid_core_last, part, level):
    @pl.when(lax.axis_index("lvl") == 0)
    def _():
        level[...] = own[...]

    @pl.when(lax.axis_index("lvl") != 0)
    def _():
        here = level_blocks(down_own, blocks_of(mid_own))
        beside = level_blocks(down_core, blocks_of(mid_core, mid_core_last))
        level[...] = stacked(*here).reshape(level.shape)
        part[...] = own_slots(matrix, (0, 1), (here, beside))


def start_near_kernel(matrix, own, down_own, down_core, mid_own, mid_core, part, level):
    @pl.when(lax.axis_index("lvl") == 0)
    def _():
        level[...] = own[...]
        part[...] = near(matrix, joined(blocks_of(own, down_core))).reshape(part.shape)

    @pl.when(lax.axis_index("lvl") != 0)
    def _():
        here = level_blocks(down_own, blocks_of(mid_own))
        beside = level_blocks(down_core, blocks_of(mid_core))
        level[...] = stacked(*here).reshape(level.shape)
        part[...] = own_slots(matrix, (0, 1), (here, beside))


def start_far_kernel(matrix, part, cross, down_cross, skewed, first):
    @pl.when(lax.axis_index("lvl") == 0)
    def _():
        first[...] = part[...] + far(matrix, joined(blocks_of(cross))).reshape(first.shape)

    @pl.when(lax.axis_index("lvl") != 0)
    def _():
        beside = level_blocks(rows_of(down_cross), rows_of(skewed))
        first[...] = part[...] + own_slots(matrix, (2,), (beside,))


def first_far_kernel(matrix, part, cross, down_cross, skewed, first):
    @pl.when(lax.axis_index("lvl") == 0)
    def _():
        first[...] = part[...] + far(matrix, joined(blocks_of(cross))).reshape(first.shape)

    @pl.when(lax.axis_index("lvl") != 0)
    def _():
        beside = level_blocks(rows_of(down_cross), rows_of(skewed))
        first[...] = part[...] + own_slots(matrix, (2,), (beside,))


def near_kernel(matrix, own, core, core_last, *rest):
    part = rest[-1]

    @pl.when(lax.axis_index("lvl") == 0)
    def _():
        part[...] = near(matrix, joined(blocks_of(own, core, core_last))).reshape(part.shape)

    @pl.when(lax.axis_index("lvl") != 0)
    def _():
        part[...] = own_slots(matrix, (0, 1), (blocks_of(own), blocks_of(core, core_last)))


def fix_kernel(matrix, level, own, part, cross, prolong, smooth, fixes):
    @pl.when(lax.axis_index("lvl") == 0)
    def _():
        fixes[...] = jnp.zeros_like(fixes)

    @pl.when(lax.axis_index("lvl") != 0)
    def _():
        second = part[...] + own_slots(matrix, (2,), (blocks_of(cross),))
        value = COEF_ZERO * level[...] + COEF_ONE * own[...] + COEF_TWO * second
        coarse = value[1]
        size = coarse.shape[0]
        up = product(prolong[:4 * size, :size], split_columns(coarse))
        low, high = value[0] + up[:size], value[2] + up[size:]
        fixes[0] = low + coarse
        fixes[1] = high + coarse
        smooth[0] = low
        smooth[1] = coarse
        smooth[2] = high


def smooth_kernel(passed, matrix, level, own, part, cross, *rest):
    smooth = rest[-1]

    @pl.when(lax.axis_index("lvl") == 0)
    def _():
        second = part[...] + far(matrix, joined(blocks_of(cross))).reshape(part.shape)
        value = COEF_ZERO * level[...] + COEF_ONE * own[...] + COEF_TWO * second
        smooth[...] = value if len(rest) == 1 else rest[0][...] + value


def solution_kernel(smooth, fixes, prolong, result):
    @pl.when(lax.axis_index("lvl") == 0)
    def _():
        result[...] = smooth[...] + product(prolong[...], joined(blocks_of(fixes))).reshape(smooth.shape)

    @pl.when(lax.axis_index("lvl") != 0)
    def _():
        result[...] = smooth[...]


def tall_kernel(matrix, restrict, tall):
    big, wide = matrix.shape[0] // 2, restrict.shape[0] // 2

    @pl.when(lax.axis_index("lvl") == 0)
    def _():
        tall[:big, :] = matrix[:big, :]
        tall[big + wide:2 * big + wide, :] = matrix[big:, :]
        for c in range(0, matrix.shape[1], big):
            right = jnp.concatenate([matrix[:big, c:c + big], matrix[big:, c:c + big]], axis=1)
            high, low = split(product(restrict[...], right))
            tall[big:big + wide, c:c + big] = high
            tall[2 * big + wide:, c:c + big] = low


def residual_near_kernel(tall, own, core, core_last, part):
    @pl.when(lax.axis_index("lvl") == 0)
    def _():
        part[...] = near(tall, joined(blocks_of(own, core, core_last)))


def residual_mid_kernel(tall, part, cross, before, mids, skewed):
    size = mids.shape[1]
    big, half = part.shape[0] - 2 * size, tall.shape[0] // 2

    @pl.when(lax.axis_index("lvl") == 0)
    def _():
        columns = 2 * (tall.shape[1] // 3)
        left = stacked(tall[big:half, columns:], tall[half + big:, columns:])
        value = part[big:, :] + product(left, joined(blocks_of(cross)))
        store_mids(before[...].reshape(2 * size, -1) - value, mids, skewed)

    @pl.when(lax.axis_index("lvl") != 0)
    def _():
        mids[...] = jnp.zeros_like(mids)
        skewed[...] = jnp.zeros_like(skewed)


def residual_far_kernel(matrix, part, cross, rhs, resid):
    big = rhs.shape[0] * rhs.shape[1]

    @pl.when(lax.axis_index("lvl") == 0)
    def _():
        value = part[:big, :] + far(matrix, joined(blocks_of(cross)))
        resid[...] = rhs[...] - value.reshape(rhs.shape)

    @pl.when(lax.axis_index("lvl") != 0)
    def _():
        resid[...] = jnp.zeros_like(resid)


def call(kernel, outs, args, anywhere=0, scratch=(), aliases={}):
    args = [pltpu.with_memory_space_constraint(a, pltpu.HBM) for a in args[:anywhere]] + list(args[anywhere:])
    spaces = [pl.BlockSpec(memory_space=pltpu.HBM)] * anywhere
    spaces += [pl.BlockSpec(memory_space=pltpu.VMEM)] * (len(args) - anywhere)
    return pl.pallas_call(
        kernel,
        out_shape=[jax.ShapeDtypeStruct(shape, dtype) for shape, dtype in outs],
        in_specs=spaces,
        out_specs=[pl.BlockSpec(memory_space=pltpu.VMEM)] * len(outs),
        scratch_shapes=scratch,
        input_output_aliases=aliases,
        compiler_params=pltpu.CompilerParams(vmem_limit_bytes=24 * 1024 * 1024),
        cost_estimate=pl.CostEstimate(flops=0, bytes_accessed=0, transcendentals=0),
    )(*args)


def swaps(rows):
    across = [0] + [r + 1 if r % 2 else r - 1 for r in range(1, rows - 1)] + [rows - 1]
    core = [(l * rows + r, l * rows + (r ^ 1)) for l in range(2) for r in range(rows)]
    cross = [(l * rows + r, l * rows + across[r]) for l in range(2) for r in range(1, rows - 1)]
    cross += [(l * rows + r, (1 - l) * rows + r) for l in range(2) for r in (0, rows - 1)]
    fine = [(r, across[r]) for r in range(1, rows - 1)] + [(0, rows - 1), (rows - 1, 0)]
    fine += [(rows + r, rows + (r ^ 1)) for r in range(rows)]
    short = [(r, across[r]) for r in range(1, rows - 1)] + [(rows + r, rows + (r ^ 1)) for r in range(2, rows - 2)]
    for end, beside in ((0, 1), (rows - 1, rows - 2)):
        short += [(end, rows + beside), (rows + beside, rows + end), (rows + end, end)]
    other = [(r, r ^ 1) for r in range(2, rows - 2)] + [(rows + r, rows + across[r]) for r in range(1, rows - 1)]
    for end, beside in ((0, 1), (rows - 1, rows - 2)):
        other += [(rows + end, end), (end, beside), (beside, rows + end)]
    level = [(l * rows + r, (1 - l) * rows + r) for l in range(2) for r in range(rows)]
    skew = [(r, rows + across[r]) for r in range(1, rows - 1)]
    skew += [(rows + r, r) for r in range(rows) if r not in (1, rows - 2)]
    for end, beside in ((0, 1), (rows - 1, rows - 2)):
        skew += [(end, beside), (rows + beside, rows + end)]
    return tuple((lambda x, pairs=pairs: lax.ppermute(x, ("lvl", "row"), pairs)) for pairs in (core, cross, fine, short, other, level, skew))


def paired(rhs, op_tiles, op_cols, link_tiles, level_links):
    core, cross, fine, short, other, level, skew = swaps(lax.axis_size("row"))
    right, tiles, links = rhs[0, 0], op_tiles[0, 0], link_tiles[0, 0]
    slots, size, width = right.shape
    blocks, pair = (right.shape, F32), ((2, size, width), F32)
    big = slots * size
    codes, goals = jnp.swapaxes(op_cols, 1, 2), jnp.swapaxes(level_links, 2, 3)
    long = ((2 * size + 8, width), F32)
    mids, skewed, payload, wide, restrict = call(
        restrict_kernel,
        [pair, long, blocks, ((2 * size + 8, width), F32), ((4 * size, big), BF16)],
        [goals, right, links],
        anywhere=3,
        scratch=[
            pltpu.SMEM(goals.shape[2:], goals.dtype),
            pltpu.VMEM(links.shape, links.dtype),
            pltpu.SemaphoreType.DMA((3,)),
        ],
    )
    down = result = matrix = prolong = tall = None
    for cycle in range(CYCLES):
        if cycle > 0:
            result_cross = short(result)
            (part,) = call(
                residual_near_kernel,
                [((big + 2 * size, width), F32)],
                [tall, result, core(result[:-1]), core(result[-1:])],
            )
            mids, skewed = call(residual_mid_kernel, [pair, long], [tall, part, result_cross, mids])
            (payload,) = call(residual_far_kernel, [blocks], [matrix, part, result_cross, right])
        mid_here, mid_cross = level(mids), skew(skewed)
        if cycle == 0:
            beyond, beside, mid_core = short(payload), [core(payload)], [core(mid_here)]
            matrix, prolong = call(
                operator_kernel,
                [((2 * big, 3 * big), BF16), ((2 * big, 2 * size), BF16)],
                [codes, goals, links, tiles],
                anywhere=4,
                scratch=[
                    pltpu.SMEM(codes.shape[1:], codes.dtype),
                    pltpu.SMEM(goals.shape[2:], goals.dtype),
                    pltpu.VMEM(links.shape, links.dtype),
                    pltpu.VMEM(tiles.shape, tiles.dtype),
                    pltpu.VMEM((slots, 3 * slots, size, size), F32),
                    pltpu.SemaphoreType.DMA((3 + slots,)),
                ],
            )
            down = payload, beside[0], other(wide)
            part, level_resid = call(
                start_near_kernel,
                [blocks, blocks],
                [matrix, payload, *down[:2], mid_here, *mid_core],
            )
            (first,) = call(
                start_far_kernel,
                [blocks],
                [matrix, part, beyond, down[2], mid_cross],
            )
            (tall,) = call(tall_kernel, [((2 * big + 4 * size, 3 * big), BF16)], [matrix, restrict])
        else:
            beyond, beside = fine(payload), [core(payload)]
            mid_core = [core(mid_here[:1]), core(mid_here[1:])]
            (part,) = call(first_fine_kernel, [blocks], [matrix, payload, *beside])
            part, level_resid = call(
                first_near_kernel,
                [blocks, blocks],
                [part, matrix, payload, *down[:2], mid_here, *mid_core],
                aliases={0: 0},
            )
            (first,) = call(first_far_kernel, [blocks], [matrix, part, beyond, down[2], mid_cross])
        first_cross = cross(first)
        (part,) = call(near_kernel, [blocks], [matrix, first, core(first[:-1]), core(first[-1:])] + ([tall] if cycle == 0 else []))
        known = [matrix, level_resid, first, part, first_cross]
        smooth, fixes = call(fix_kernel, [blocks, pair], [*known, prolong])
        fixes = level(fixes)
        before = [] if cycle == 0 else [result]
        (smooth,) = call(smooth_kernel, [blocks], [smooth, *known, *before], aliases={0: 0})
        (result,) = call(solution_kernel, [blocks], [smooth, fixes, prolong])
    return result[None, None]


def body(rhs, *rest):
    rows = lax.axis_size("row")
    square = rhs.shape[-1] == rhs.shape[-2]
    plan = paired if lax.axis_size("lvl") == 2 and rows % 2 == 0 and rows > 2 and square else per_device
    return plan(rhs, *rest)


def solution(mesh):
    placed = (
        P("lvl", "row", None, None, None),
        P("lvl", "row", None, None, None, None),
        P("lvl", "row", None, None),
        P("lvl", "row", None, None, None, None),
        P("lvl", "row", None, None),
    )
    return jax.shard_map(
        body,
        mesh=mesh,
        in_specs=placed,
        out_specs=P("lvl", "row", None, None, None),
        check_vma=False,
    )
```

```python
import functools

import jax
import jax.numpy as jnp
from jax import lax
from jax.experimental import pallas as pl
from jax.experimental.pallas import tpu as pltpu
from jax.sharding import PartitionSpec as P

CYCLES = 2


HIGH = lax.Precision.HIGHEST
COEF_ZERO = 0.9
COEF_ONE = -0.36
COEF_TWO = 0.05
F32 = jnp.float32
BF16 = jnp.bfloat16


def extended(block, sides, width):
    for axis, dim in sides:
        count = lax.axis_size(axis)
        forward = [(i, i + 1) for i in range(count - 1)]
        backward = [(target, source) for source, target in forward]
        low = lax.ppermute(
            lax.slice_in_dim(block, block.shape[dim] - width, None, axis=dim), axis, forward
        )
        high = lax.ppermute(lax.slice_in_dim(block, 0, width, axis=dim), axis, backward)
        block = jnp.concatenate([low, block, high], axis=dim)
    return block


def broadcast(block, axis, source):
    block = jnp.where(lax.axis_index(axis) == source, block, jnp.zeros_like(block))
    return lax.psum(block, axis)


def apply_operator(field, tiles, columns, keep):
    slots = field.shape[0]
    padded = extended(field[None], (("row", 0),), 1)
    candidates = padded.reshape((3 * slots,) + field.shape[1:])
    picked = candidates[columns]
    image = jnp.einsum("sjab,sjbn->san", tiles, picked, precision=HIGH)
    return image * keep[:, None, None]


def per_device(rhs, op_tiles, op_cols, link_tiles, level_links):
    n_lvl = lax.axis_size("lvl")
    fine_lvls = 5 * n_lvl // 8
    mid_lvls = max(n_lvl - fine_lvls - 1, 1)
    lvl_here = lax.axis_index("lvl")
    right = rhs[0, 0]
    tiles = op_tiles[0, 0]
    columns = op_cols[0, 0]
    links = link_tiles[0, 0]
    targets = level_links[0, 0]
    slots = right.shape[0]
    slot_ids = jnp.arange(slots)
    pair_ids = jnp.arange(2)
    is_fine = lvl_here < fine_lvls
    is_mid = (lvl_here >= fine_lvls) & (lvl_here < fine_lvls + mid_lvls)
    is_coarse = lvl_here == n_lvl - 1
    fine_keep = jnp.where(is_fine & (slot_ids >= 0), 1.0, 0.0).astype(jnp.float32)
    mid_keep = jnp.where(is_mid & ((slot_ids == 0) | (slot_ids == 2)), 1.0, 0.0).astype(jnp.float32)
    coarse_keep = jnp.where(is_coarse & (slot_ids == 1), 1.0, 0.0).astype(jnp.float32)
    all_keep = fine_keep + mid_keep + coarse_keep
    mid_flag = jnp.where(is_mid, 1.0, 0.0).astype(jnp.float32)
    place = (slot_ids[:, None] == 2 * pair_ids[None, :]).astype(jnp.float32) * mid_flag
    lvl_ids = jnp.arange(n_lvl)

    def lvl_table(target):
        by_lvl = (target[:, None] // 2 + fine_lvls == lvl_ids[None, :]).astype(jnp.float32)
        by_pair = (target[:, None] % 2 == pair_ids[None, :]).astype(jnp.float32)
        return by_lvl[:, :, None] * by_pair[:, None, :] * fine_keep[:, None, None]

    to_lvl = lvl_table(targets[:, 0])
    from_lvl = lvl_table(targets[:, 1])
    mid_restrict = jnp.stack([links[0, 0], links[2, 0]])
    mid_prolong = jnp.stack([links[0, 1], links[2, 1]])
    solution = jnp.zeros_like(right)
    mid_fix = jnp.zeros((2,) + right.shape[1:], jnp.float32)
    coarse_fix = jnp.zeros_like(right[0])
    for cycle in range(CYCLES):
        if cycle == 0:
            resid = right * fine_keep[:, None, None]
        else:
            resid = (right - apply_operator(solution, tiles, columns, all_keep)) * fine_keep[
                :, None, None
            ]
        terms = jnp.einsum("sab,sbn->san", links[:, 0], resid, precision=HIGH)
        dense = jnp.einsum("slm,san->lman", to_lvl, terms, precision=HIGH)
        mid_resid = lax.psum_scatter(dense, "lvl", scatter_dimension=0, tiled=True)[0] * mid_flag
        mid_part = jnp.einsum("mab,mbn->an", mid_restrict, mid_resid, precision=HIGH) * mid_flag
        fine_part = 0.5 * jnp.sum(terms * fine_keep[:, None, None], axis=0)
        coarse_resid = lax.psum(mid_part + fine_part, "lvl")
        level_resid = resid + jnp.einsum("sm,man->san", place, mid_resid, precision=HIGH)
        level_resid = level_resid + coarse_keep[:, None, None] * coarse_resid[None]
        first = apply_operator(level_resid, tiles, columns, all_keep)
        second = apply_operator(first, tiles, columns, all_keep)
        smooth = COEF_ZERO * level_resid + COEF_ONE * first + COEF_TWO * second
        coarse_fix = broadcast(smooth[1], "lvl", n_lvl - 1)
        mid_fix = jnp.stack([smooth[0], smooth[2]]) + jnp.einsum(
            "mab,bn->man", mid_prolong, coarse_fix, precision=HIGH
        )
        gathered = lax.all_gather(mid_fix[None], "lvl", axis=0, tiled=True)
        chosen = jnp.einsum("slm,lman->san", from_lvl, gathered, precision=HIGH)
        chosen = chosen + coarse_fix[None]
        fine_fix = smooth + jnp.einsum("sab,sbn->san", links[:, 1], chosen, precision=HIGH)
        solution = solution + fine_fix * fine_keep[:, None, None]
    levels = solution * fine_keep[:, None, None] + jnp.einsum(
        "sm,man->san", place, mid_fix, precision=HIGH
    )
    levels = levels + coarse_keep[:, None, None] * coarse_fix[None]
    return levels[None, None]


def split(value):
    high = value.astype(BF16)
    return high, (value - high.astype(F32)).astype(BF16)


def split_rows(value):
    return jnp.concatenate(split(value), axis=0)


def split_columns(value):
    return jnp.concatenate(split(value), axis=1)


def product(left, right):
    full = jnp.dot(left, right, preferred_element_type=F32)
    rows, columns = full.shape[0] // 2, full.shape[1] // 2
    small = full[rows:, :columns] + full[:rows, columns:] + full[rows:, columns:]
    return full[:rows, :columns] + small


def stacked(*blocks):
    return jnp.concatenate(blocks, axis=0)


def store_mids(value, mids, skewed):
    mids[...] = value.reshape(mids.shape)
    skewed[:value.shape[0], :] = value
    skewed[value.shape[0]:, :] = jnp.zeros_like(skewed[value.shape[0]:, :])


def restrict_kernel(targets_in, rhs_in, links_in, mids, skewed, payload, wide, restrict, targets, links, sems):
    size = payload.shape[-1]
    slots = payload.shape[0]
    fetch_targets = pltpu.make_async_copy(targets_in.at[0, 0], targets, sems.at[0])
    fetch_links = pltpu.make_async_copy(links_in, links, sems.at[1])
    fetch_rhs = pltpu.make_async_copy(rhs_in, payload, sems.at[2])
    fetch_targets.start()
    fetch_links.start()

    @pl.when(lax.axis_index("lvl") == 0)
    def _():
        fetch_rhs.start()
        fetch_targets.wait()
        fetch_links.wait()
        for s in range(slots):
            for k in range(2):
                down = jnp.where(targets[0, s] == k, links[s, 0], 0.0)
                high, low = split(down)
                restrict[k * size:(k + 1) * size, s * size:(s + 1) * size] = high
                restrict[(2 + k) * size:(3 + k) * size, s * size:(s + 1) * size] = low
        fetch_rhs.wait()
        right = split_columns(payload[...].reshape(slots * size, size))
        store_mids(product(restrict[...], right), mids, skewed)
        wide[...] = jnp.zeros_like(wide)

    @pl.when(lax.axis_index("lvl") != 0)
    def _():
        fetch_targets.wait()
        fetch_links.wait()
        payload[0] = links[0, 0]
        payload[1] = links[2, 0]
        payload[2] = jnp.zeros_like(payload[2])
        wide[:2 * size, :] = stacked(links[0, 0], links[2, 0])
        wide[2 * size:, :] = jnp.zeros_like(wide[2 * size:, :])
        mids[...] = jnp.zeros_like(mids)
        skewed[...] = jnp.zeros_like(skewed)


def operator_kernel(columns_in, targets_in, links_in, tiles_in, matrix, prolong, columns, targets, links, tiles, gathered, sems):
    slots, count, size = tiles.shape[0], tiles.shape[1], tiles.shape[-1]
    fetch_columns = pltpu.make_async_copy(columns_in.at[0], columns, sems.at[0])
    fetch_targets = pltpu.make_async_copy(targets_in.at[0, 0], targets, sems.at[1])
    fetch_links = pltpu.make_async_copy(links_in, links, sems.at[2])
    fetch_tiles = [pltpu.make_async_copy(tiles_in.at[s], tiles.at[s], sems.at[3 + s]) for s in range(slots)]
    for fetch in (fetch_columns, fetch_targets, *fetch_tiles, fetch_links):
        fetch.start()
    row = lax.axis_index("row")
    odd = lax.rem(row, 2)
    inner = (row > 0) & (row < lax.axis_size("row") - 1)
    gathered[...] = jnp.zeros_like(gathered)
    fetch_columns.wait()
    fetch_targets.wait()
    for s in range(slots):
        fetch_tiles[s].wait()
        for j in range(count):
            code = columns[s, 0, j]
            step = code // slots
            slot = code - slots * step
            side = jnp.where(step == 1, 0, jnp.where(step == 2 * (1 - odd), 1, 2))
            gathered[s, side * slots + slot] += tiles[s, j]
        for c in range(3 * slots):
            block = gathered[s, c]
            if c >= 2 * slots:
                block = jnp.where(inner, block, 0.0)
            high, low = split(block)
            matrix[s * size:(s + 1) * size, c * size:(c + 1) * size] = high
            matrix[(slots + s) * size:(slots + s + 1) * size, c * size:(c + 1) * size] = low
    fetch_links.wait()

    @pl.when(lax.axis_index("lvl") == 0)
    def _():
        for s in range(slots):
            for k in range(2):
                up = jnp.where(targets[1, s] == k, links[s, 1], 0.0)
                high, low = split(up)
                prolong[s * size:(s + 1) * size, k * size:(k + 1) * size] = high
                prolong[(slots + s) * size:(slots + s + 1) * size, k * size:(k + 1) * size] = low

    @pl.when(lax.axis_index("lvl") != 0)
    def _():
        prolong[:4 * size, :size] = split_rows(stacked(links[0, 1], links[2, 1]))
        at, big = (2 * slots + 1) * size, slots * size
        coarse = [matrix[first + size:first + 2 * size, at:at + size] for first in (0, big)]
        lifted = product(prolong[:4 * size, :size], jnp.concatenate(coarse, axis=1))
        prolong[:4 * size, size:] = split_rows(lifted)


def joined(blocks):
    return split_columns(stacked(*blocks))


def blocks_of(*refs):
    return [ref[s] for ref in refs for s in range(ref.shape[0])]


def own_slots(matrix, sides, groups):
    size = groups[0][0].shape[0]
    slots = len(groups[0])
    parts = []
    for s in range(slots):
        columns = [slice((side * slots + s) * size, (side * slots + s + 1) * size) for side in sides]
        high = [matrix[s * size:(s + 1) * size, c] for c in columns]
        low = [matrix[(slots + s) * size:(slots + s + 1) * size, c] for c in columns]
        left = stacked(jnp.concatenate(high, axis=1), jnp.concatenate(low, axis=1))
        parts.append(product(left, joined([group[s] for group in groups])))
    return stacked(*parts).reshape(slots, size, -1)


def near(matrix, field):
    columns = 2 * (matrix.shape[1] // 3)
    return product(matrix[:, :columns], field)


def far(matrix, field):
    columns = 2 * (matrix.shape[1] // 3)
    return product(matrix[:, columns:], field)


def level_blocks(down, mid):
    left = split_rows(jnp.concatenate([down[0], down[1]], axis=1))
    coarse = product(left, joined((mid[0], mid[1]))) + 0.5 * (mid[0] + mid[1])
    return [mid[0], coarse, mid[1]]


def rows_of(ref):
    size = ref.shape[-1]
    return [ref[k * size:(k + 1) * size, :] for k in range(2)]


def first_fine_kernel(matrix, own, *rest):
    *core, part = rest

    @pl.when(lax.axis_index("lvl") == 0)
    def _():
        part[...] = near(matrix, joined(blocks_of(own, *core))).reshape(part.shape)


def first_near_kernel(fine_part, matrix, own, down_own, down_core, mid_own, mid_core, mid_core_last, part, level):
    @pl.when(lax.axis_index("lvl") == 0)
    def _():
        level[...] = own[...]

    @pl.when(lax.axis_index("lvl") != 0)
    def _():
        here = level_blocks(down_own, blocks_of(mid_own))
        beside = level_blocks(down_core, blocks_of(mid_core, mid_core_last))
        level[...] = stacked(*here).reshape(level.shape)
        part[...] = own_slots(matrix, (0, 1), (here, beside))


def start_near_kernel(matrix, own, down_own, down_core, mid_own, mid_core, part, level):
    @pl.when(lax.axis_index("lvl") == 0)
    def _():
        level[...] = own[...]
        part[...] = near(matrix, joined(blocks_of(own, down_core))).reshape(part.shape)

    @pl.when(lax.axis_index("lvl") != 0)
    def _():
        here = level_blocks(down_own, blocks_of(mid_own))
        beside = level_blocks(down_core, blocks_of(mid_core))
        level[...] = stacked(*here).reshape(level.shape)
        part[...] = own_slots(matrix, (0, 1), (here, beside))


def start_far_kernel(matrix, part, cross, down_cross, skewed, first):
    @pl.when(lax.axis_index("lvl") == 0)
    def _():
        first[...] = part[...] + far(matrix, joined(blocks_of(cross))).reshape(first.shape)

    @pl.when(lax.axis_index("lvl") != 0)
    def _():
        beside = level_blocks(rows_of(down_cross), rows_of(skewed))
        first[...] = part[...] + own_slots(matrix, (2,), (beside,))


def first_far_kernel(matrix, part, cross, down_cross, skewed, first):
    @pl.when(lax.axis_index("lvl") == 0)
    def _():
        first[...] = part[...] + far(matrix, joined(blocks_of(cross))).reshape(first.shape)

    @pl.when(lax.axis_index("lvl") != 0)
    def _():
        beside = level_blocks(rows_of(down_cross), rows_of(skewed))
        first[...] = part[...] + own_slots(matrix, (2,), (beside,))


def near_kernel(matrix, own, core, core_last, level, prolong, *rest):
    part, lift = rest[-2:]

    @pl.when(lax.axis_index("lvl") == 0)
    def _():
        part[...] = near(matrix, joined(blocks_of(own, core, core_last))).reshape(part.shape)

    @pl.when(lax.axis_index("lvl") != 0)
    def _():
        size = own.shape[1]
        beside = own_slots(matrix, (0, 1), (blocks_of(own), blocks_of(core, core_last)))
        value = COEF_ZERO * level[...] + COEF_ONE * own[...] + COEF_TWO * beside
        up = product(prolong[:4 * size, :size], split_columns(value[1]))
        part[...] = value
        lift[0] = value[0] + up[:size]
        lift[1] = value[2] + up[size:]


def fix_kernel(matrix, part, lift, cross, prolong, smooth, fixes):
    @pl.when(lax.axis_index("lvl") == 0)
    def _():
        fixes[...] = jnp.zeros_like(fixes)

    @pl.when(lax.axis_index("lvl") != 0)
    def _():
        size = cross.shape[1]
        up = product(prolong[:4 * size, size:], split_columns(cross[1]))
        beyond = own_slots(matrix, (2,), (blocks_of(cross),))
        coarse = part[1] + COEF_TWO * beyond[1]
        low = lift[0] + COEF_TWO * (beyond[0] + up[:size])
        high = lift[1] + COEF_TWO * (beyond[2] + up[size:])
        fixes[0] = low + coarse
        fixes[1] = high + coarse
        smooth[0] = low
        smooth[1] = coarse
        smooth[2] = high


def smooth_kernel(passed, matrix, level, own, part, cross, *rest):
    smooth = rest[-1]

    @pl.when(lax.axis_index("lvl") == 0)
    def _():
        second = part[...] + far(matrix, joined(blocks_of(cross))).reshape(part.shape)
        value = COEF_ZERO * level[...] + COEF_ONE * own[...] + COEF_TWO * second
        smooth[...] = value if len(rest) == 1 else rest[0][...] + value


def solution_kernel(smooth, fixes, prolong, result):
    @pl.when(lax.axis_index("lvl") == 0)
    def _():
        result[...] = smooth[...] + product(prolong[...], joined(blocks_of(fixes))).reshape(smooth.shape)

    @pl.when(lax.axis_index("lvl") != 0)
    def _():
        result[...] = smooth[...]


def tall_kernel(matrix, restrict, tall):
    big, wide = matrix.shape[0] // 2, restrict.shape[0] // 2

    @pl.when(lax.axis_index("lvl") == 0)
    def _():
        tall[:big, :] = matrix[:big, :]
        tall[big + wide:2 * big + wide, :] = matrix[big:, :]
        for c in range(0, matrix.shape[1], big):
            right = jnp.concatenate([matrix[:big, c:c + big], matrix[big:, c:c + big]], axis=1)
            high, low = split(product(restrict[...], right))
            tall[big:big + wide, c:c + big] = high
            tall[2 * big + wide:, c:c + big] = low


def residual_near_kernel(tall, own, core, core_last, part):
    @pl.when(lax.axis_index("lvl") == 0)
    def _():
        part[...] = near(tall, joined(blocks_of(own, core, core_last)))


def residual_mid_kernel(tall, part, cross, before, mids, skewed):
    size = mids.shape[1]
    big, half = part.shape[0] - 2 * size, tall.shape[0] // 2

    @pl.when(lax.axis_index("lvl") == 0)
    def _():
        columns = 2 * (tall.shape[1] // 3)
        left = stacked(tall[big:half, columns:], tall[half + big:, columns:])
        value = part[big:, :] + product(left, joined(blocks_of(cross)))
        store_mids(before[...].reshape(2 * size, -1) - value, mids, skewed)

    @pl.when(lax.axis_index("lvl") != 0)
    def _():
        mids[...] = jnp.zeros_like(mids)
        skewed[...] = jnp.zeros_like(skewed)


def residual_far_kernel(matrix, part, cross, rhs, resid):
    big = rhs.shape[0] * rhs.shape[1]

    @pl.when(lax.axis_index("lvl") == 0)
    def _():
        value = part[:big, :] + far(matrix, joined(blocks_of(cross)))
        resid[...] = rhs[...] - value.reshape(rhs.shape)

    @pl.when(lax.axis_index("lvl") != 0)
    def _():
        resid[...] = jnp.zeros_like(resid)


def call(kernel, outs, args, anywhere=0, scratch=(), aliases={}):
    args = [pltpu.with_memory_space_constraint(a, pltpu.HBM) for a in args[:anywhere]] + list(args[anywhere:])
    spaces = [pl.BlockSpec(memory_space=pltpu.HBM)] * anywhere
    spaces += [pl.BlockSpec(memory_space=pltpu.VMEM)] * (len(args) - anywhere)
    return pl.pallas_call(
        kernel,
        out_shape=[jax.ShapeDtypeStruct(shape, dtype) for shape, dtype in outs],
        in_specs=spaces,
        out_specs=[pl.BlockSpec(memory_space=pltpu.VMEM)] * len(outs),
        scratch_shapes=scratch,
        input_output_aliases=aliases,
        compiler_params=pltpu.CompilerParams(vmem_limit_bytes=24 * 1024 * 1024),
        cost_estimate=pl.CostEstimate(flops=0, bytes_accessed=0, transcendentals=0),
    )(*args)


def swaps(rows):
    across = [0] + [r + 1 if r % 2 else r - 1 for r in range(1, rows - 1)] + [rows - 1]
    core = [(l * rows + r, l * rows + (r ^ 1)) for l in range(2) for r in range(rows)]
    cross = [(l * rows + r, l * rows + across[r]) for l in range(2) for r in range(1, rows - 1)]
    cross += [(l * rows + r, (1 - l) * rows + r) for l in range(2) for r in (0, rows - 1)]
    fine = [(r, across[r]) for r in range(1, rows - 1)] + [(0, rows - 1), (rows - 1, 0)]
    fine += [(rows + r, rows + (r ^ 1)) for r in range(rows)]
    short = [(r, across[r]) for r in range(1, rows - 1)] + [(rows + r, rows + (r ^ 1)) for r in range(2, rows - 2)]
    for end, beside in ((0, 1), (rows - 1, rows - 2)):
        short += [(end, rows + beside), (rows + beside, rows + end), (rows + end, end)]
    other = [(r, r ^ 1) for r in range(2, rows - 2)] + [(rows + r, rows + across[r]) for r in range(1, rows - 1)]
    for end, beside in ((0, 1), (rows - 1, rows - 2)):
        other += [(rows + end, end), (end, beside), (beside, rows + end)]
    level = [(l * rows + r, (1 - l) * rows + r) for l in range(2) for r in range(rows)]
    skew = [(r, rows + across[r]) for r in range(1, rows - 1)]
    skew += [(rows + r, r) for r in range(rows) if r not in (1, rows - 2)]
    for end, beside in ((0, 1), (rows - 1, rows - 2)):
        skew += [(end, beside), (rows + beside, rows + end)]
    return tuple((lambda x, pairs=pairs: lax.ppermute(x, ("lvl", "row"), pairs)) for pairs in (core, cross, fine, short, other, level, skew))


def paired(rhs, op_tiles, op_cols, link_tiles, level_links):
    core, cross, fine, short, other, level, skew = swaps(lax.axis_size("row"))
    right, tiles, links = rhs[0, 0], op_tiles[0, 0], link_tiles[0, 0]
    slots, size, width = right.shape
    blocks, pair = (right.shape, F32), ((2, size, width), F32)
    big = slots * size
    codes, goals = jnp.swapaxes(op_cols, 1, 2), jnp.swapaxes(level_links, 2, 3)
    long = ((2 * size + 8, width), F32)
    mids, skewed, payload, wide, restrict = call(
        restrict_kernel,
        [pair, long, blocks, ((2 * size + 8, width), F32), ((4 * size, big), BF16)],
        [goals, right, links],
        anywhere=3,
        scratch=[
            pltpu.SMEM(goals.shape[2:], goals.dtype),
            pltpu.VMEM(links.shape, links.dtype),
            pltpu.SemaphoreType.DMA((3,)),
        ],
    )
    down = result = matrix = prolong = tall = None
    for cycle in range(CYCLES):
        if cycle > 0:
            result_cross = short(result)
            (part,) = call(
                residual_near_kernel,
                [((big + 2 * size, width), F32)],
                [tall, result, core(result[:-1]), core(result[-1:])],
            )
            mids, skewed = call(residual_mid_kernel, [pair, long], [tall, part, result_cross, mids])
            (payload,) = call(residual_far_kernel, [blocks], [matrix, part, result_cross, right])
        mid_here, mid_cross = level(mids), skew(skewed)
        if cycle == 0:
            beyond, beside, mid_core = short(payload), [core(payload)], [core(mid_here)]
            matrix, prolong = call(
                operator_kernel,
                [((2 * big, 3 * big), BF16), ((2 * big, 2 * size), BF16)],
                [codes, goals, links, tiles],
                anywhere=4,
                scratch=[
                    pltpu.SMEM(codes.shape[1:], codes.dtype),
                    pltpu.SMEM(goals.shape[2:], goals.dtype),
                    pltpu.VMEM(links.shape, links.dtype),
                    pltpu.VMEM(tiles.shape, tiles.dtype),
                    pltpu.VMEM((slots, 3 * slots, size, size), F32),
                    pltpu.SemaphoreType.DMA((3 + slots,)),
                ],
            )
            down = payload, beside[0], other(wide)
            part, level_resid = call(
                start_near_kernel,
                [blocks, blocks],
                [matrix, payload, *down[:2], mid_here, *mid_core],
            )
            (first,) = call(
                start_far_kernel,
                [blocks],
                [matrix, part, beyond, down[2], mid_cross],
            )
            (tall,) = call(tall_kernel, [((2 * big + 4 * size, 3 * big), BF16)], [matrix, restrict])
        else:
            beyond, beside = fine(payload), [core(payload)]
            mid_core = [core(mid_here[:1]), core(mid_here[1:])]
            (part,) = call(first_fine_kernel, [blocks], [matrix, payload, *beside])
            part, level_resid = call(
                first_near_kernel,
                [blocks, blocks],
                [part, matrix, payload, *down[:2], mid_here, *mid_core],
                aliases={0: 0},
            )
            (first,) = call(first_far_kernel, [blocks], [matrix, part, beyond, down[2], mid_cross])
        first_cross = cross(first)
        halves = [core(first[:-1]), core(first[-1:])]
        more = [tall] if cycle == 0 else []
        part, lift = call(near_kernel, [blocks, pair], [matrix, first, *halves, level_resid, prolong, *more])
        known = [matrix, level_resid, first, part, first_cross]
        smooth, fixes = call(fix_kernel, [blocks, pair], [matrix, part, lift, first_cross, prolong])
        fixes = level(fixes)
        before = [] if cycle == 0 else [result]
        (smooth,) = call(smooth_kernel, [blocks], [smooth, *known, *before], aliases={0: 0})
        (result,) = call(solution_kernel, [blocks], [smooth, fixes, prolong])
    return result[None, None]


def body(rhs, *rest):
    rows = lax.axis_size("row")
    square = rhs.shape[-1] == rhs.shape[-2]
    plan = paired if lax.axis_size("lvl") == 2 and rows % 2 == 0 and rows > 2 and square else per_device
    return plan(rhs, *rest)


def solution(mesh):
    placed = (
        P("lvl", "row", None, None, None),
        P("lvl", "row", None, None, None, None),
        P("lvl", "row", None, None),
        P("lvl", "row", None, None, None, None),
        P("lvl", "row", None, None),
    )
    return jax.shard_map(
        body,
        mesh=mesh,
        in_specs=placed,
        out_specs=P("lvl", "row", None, None, None),
        check_vma=False,
    )
```

```python
import functools

import jax
import jax.numpy as jnp
from jax import lax
from jax.experimental import pallas as pl
from jax.experimental.pallas import tpu as pltpu
from jax.sharding import PartitionSpec as P

CYCLES = 2


HIGH = lax.Precision.HIGHEST
COEF_ZERO = 0.9
COEF_ONE = -0.36
COEF_TWO = 0.05
F32 = jnp.float32
BF16 = jnp.bfloat16


def extended(block, sides, width):
    for axis, dim in sides:
        count = lax.axis_size(axis)
        forward = [(i, i + 1) for i in range(count - 1)]
        backward = [(target, source) for source, target in forward]
        low = lax.ppermute(
            lax.slice_in_dim(block, block.shape[dim] - width, None, axis=dim), axis, forward
        )
        high = lax.ppermute(lax.slice_in_dim(block, 0, width, axis=dim), axis, backward)
        block = jnp.concatenate([low, block, high], axis=dim)
    return block


def broadcast(block, axis, source):
    block = jnp.where(lax.axis_index(axis) == source, block, jnp.zeros_like(block))
    return lax.psum(block, axis)


def apply_operator(field, tiles, columns, keep):
    slots = field.shape[0]
    padded = extended(field[None], (("row", 0),), 1)
    candidates = padded.reshape((3 * slots,) + field.shape[1:])
    picked = candidates[columns]
    image = jnp.einsum("sjab,sjbn->san", tiles, picked, precision=HIGH)
    return image * keep[:, None, None]


def per_device(rhs, op_tiles, op_cols, link_tiles, level_links):
    n_lvl = lax.axis_size("lvl")
    fine_lvls = 5 * n_lvl // 8
    mid_lvls = max(n_lvl - fine_lvls - 1, 1)
    lvl_here = lax.axis_index("lvl")
    right = rhs[0, 0]
    tiles = op_tiles[0, 0]
    columns = op_cols[0, 0]
    links = link_tiles[0, 0]
    targets = level_links[0, 0]
    slots = right.shape[0]
    slot_ids = jnp.arange(slots)
    pair_ids = jnp.arange(2)
    is_fine = lvl_here < fine_lvls
    is_mid = (lvl_here >= fine_lvls) & (lvl_here < fine_lvls + mid_lvls)
    is_coarse = lvl_here == n_lvl - 1
    fine_keep = jnp.where(is_fine & (slot_ids >= 0), 1.0, 0.0).astype(jnp.float32)
    mid_keep = jnp.where(is_mid & ((slot_ids == 0) | (slot_ids == 2)), 1.0, 0.0).astype(jnp.float32)
    coarse_keep = jnp.where(is_coarse & (slot_ids == 1), 1.0, 0.0).astype(jnp.float32)
    all_keep = fine_keep + mid_keep + coarse_keep
    mid_flag = jnp.where(is_mid, 1.0, 0.0).astype(jnp.float32)
    place = (slot_ids[:, None] == 2 * pair_ids[None, :]).astype(jnp.float32) * mid_flag
    lvl_ids = jnp.arange(n_lvl)

    def lvl_table(target):
        by_lvl = (target[:, None] // 2 + fine_lvls == lvl_ids[None, :]).astype(jnp.float32)
        by_pair = (target[:, None] % 2 == pair_ids[None, :]).astype(jnp.float32)
        return by_lvl[:, :, None] * by_pair[:, None, :] * fine_keep[:, None, None]

    to_lvl = lvl_table(targets[:, 0])
    from_lvl = lvl_table(targets[:, 1])
    mid_restrict = jnp.stack([links[0, 0], links[2, 0]])
    mid_prolong = jnp.stack([links[0, 1], links[2, 1]])
    solution = jnp.zeros_like(right)
    mid_fix = jnp.zeros((2,) + right.shape[1:], jnp.float32)
    coarse_fix = jnp.zeros_like(right[0])
    for cycle in range(CYCLES):
        if cycle == 0:
            resid = right * fine_keep[:, None, None]
        else:
            resid = (right - apply_operator(solution, tiles, columns, all_keep)) * fine_keep[
                :, None, None
            ]
        terms = jnp.einsum("sab,sbn->san", links[:, 0], resid, precision=HIGH)
        dense = jnp.einsum("slm,san->lman", to_lvl, terms, precision=HIGH)
        mid_resid = lax.psum_scatter(dense, "lvl", scatter_dimension=0, tiled=True)[0] * mid_flag
        mid_part = jnp.einsum("mab,mbn->an", mid_restrict, mid_resid, precision=HIGH) * mid_flag
        fine_part = 0.5 * jnp.sum(terms * fine_keep[:, None, None], axis=0)
        coarse_resid = lax.psum(mid_part + fine_part, "lvl")
        level_resid = resid + jnp.einsum("sm,man->san", place, mid_resid, precision=HIGH)
        level_resid = level_resid + coarse_keep[:, None, None] * coarse_resid[None]
        first = apply_operator(level_resid, tiles, columns, all_keep)
        second = apply_operator(first, tiles, columns, all_keep)
        smooth = COEF_ZERO * level_resid + COEF_ONE * first + COEF_TWO * second
        coarse_fix = broadcast(smooth[1], "lvl", n_lvl - 1)
        mid_fix = jnp.stack([smooth[0], smooth[2]]) + jnp.einsum(
            "mab,bn->man", mid_prolong, coarse_fix, precision=HIGH
        )
        gathered = lax.all_gather(mid_fix[None], "lvl", axis=0, tiled=True)
        chosen = jnp.einsum("slm,lman->san", from_lvl, gathered, precision=HIGH)
        chosen = chosen + coarse_fix[None]
        fine_fix = smooth + jnp.einsum("sab,sbn->san", links[:, 1], chosen, precision=HIGH)
        solution = solution + fine_fix * fine_keep[:, None, None]
    levels = solution * fine_keep[:, None, None] + jnp.einsum(
        "sm,man->san", place, mid_fix, precision=HIGH
    )
    levels = levels + coarse_keep[:, None, None] * coarse_fix[None]
    return levels[None, None]


def split(value):
    high = value.astype(BF16)
    return high, (value - high.astype(F32)).astype(BF16)


def split_rows(value):
    return jnp.concatenate(split(value), axis=0)


def split_columns(value):
    return jnp.concatenate(split(value), axis=1)


def product(left, right):
    full = jnp.dot(left, right, preferred_element_type=F32)
    rows, columns = full.shape[0] // 2, full.shape[1] // 2
    small = full[rows:, :columns] + full[:rows, columns:] + full[rows:, columns:]
    return full[:rows, :columns] + small


def stacked(*blocks):
    return jnp.concatenate(blocks, axis=0)


def store_mids(value, mids, skewed):
    mids[...] = value.reshape(mids.shape)
    skewed[:value.shape[0], :] = value
    skewed[value.shape[0]:, :] = jnp.zeros_like(skewed[value.shape[0]:, :])


def restrict_kernel(targets_in, rhs_in, links_in, mids, skewed, payload, wide, restrict, targets, links, sems):
    size = payload.shape[-1]
    slots = payload.shape[0]
    fetch_targets = pltpu.make_async_copy(targets_in.at[0, 0], targets, sems.at[0])
    fetch_links = pltpu.make_async_copy(links_in.at[:, 0], links, sems.at[1])
    fetch_rhs = pltpu.make_async_copy(rhs_in, payload, sems.at[2])
    fetch_targets.start()
    fetch_links.start()

    @pl.when(lax.axis_index("lvl") == 0)
    def _():
        fetch_rhs.start()
        fetch_targets.wait()
        fetch_links.wait()
        for s in range(slots):
            for k in range(2):
                down = jnp.where(targets[0, s] == k, links[s], 0.0)
                high, low = split(down)
                restrict[k * size:(k + 1) * size, s * size:(s + 1) * size] = high
                restrict[(2 + k) * size:(3 + k) * size, s * size:(s + 1) * size] = low
        fetch_rhs.wait()
        right = split_columns(payload[...].reshape(slots * size, size))
        store_mids(product(restrict[...], right), mids, skewed)
        wide[...] = jnp.zeros_like(wide)

    @pl.when(lax.axis_index("lvl") != 0)
    def _():
        fetch_targets.wait()
        fetch_links.wait()
        payload[0] = links[0]
        payload[1] = links[2]
        payload[2] = jnp.zeros_like(payload[2])
        wide[:2 * size, :] = stacked(links[0], links[2])
        wide[2 * size:, :] = jnp.zeros_like(wide[2 * size:, :])
        mids[...] = jnp.zeros_like(mids)
        skewed[...] = jnp.zeros_like(skewed)


def operator_kernel(columns_in, targets_in, links_in, tiles_in, matrix, prolong, columns, targets, links, tiles, gathered, sems):
    slots, count, size = tiles.shape[0], tiles.shape[1], tiles.shape[-1]
    fetch_columns = pltpu.make_async_copy(columns_in.at[0], columns, sems.at[0])
    fetch_targets = pltpu.make_async_copy(targets_in.at[0, 0], targets, sems.at[1])
    fetch_links = pltpu.make_async_copy(links_in, links, sems.at[2])
    fetch_tiles = [pltpu.make_async_copy(tiles_in.at[s], tiles.at[s], sems.at[3 + s]) for s in range(slots)]
    for fetch in (fetch_columns, fetch_targets, *fetch_tiles, fetch_links):
        fetch.start()
    row = lax.axis_index("row")
    odd = lax.rem(row, 2)
    inner = (row > 0) & (row < lax.axis_size("row") - 1)
    gathered[...] = jnp.zeros_like(gathered)
    fetch_columns.wait()
    fetch_targets.wait()
    for s in range(slots):
        fetch_tiles[s].wait()
        for j in range(count):
            code = columns[s, 0, j]
            step = code // slots
            slot = code - slots * step
            side = jnp.where(step == 1, 0, jnp.where(step == 2 * (1 - odd), 1, 2))
            gathered[s, side * slots + slot] += tiles[s, j]
        for c in range(3 * slots):
            block = gathered[s, c]
            if c >= 2 * slots:
                block = jnp.where(inner, block, 0.0)
            high, low = split(block)
            matrix[s * size:(s + 1) * size, c * size:(c + 1) * size] = high
            matrix[(slots + s) * size:(slots + s + 1) * size, c * size:(c + 1) * size] = low
    fetch_links.wait()

    @pl.when(lax.axis_index("lvl") == 0)
    def _():
        for s in range(slots):
            for k in range(2):
                up = jnp.where(targets[1, s] == k, links[s, 1], 0.0)
                high, low = split(up)
                prolong[s * size:(s + 1) * size, k * size:(k + 1) * size] = high
                prolong[(slots + s) * size:(slots + s + 1) * size, k * size:(k + 1) * size] = low

    @pl.when(lax.axis_index("lvl") != 0)
    def _():
        prolong[:4 * size, :size] = split_rows(stacked(links[0, 1], links[2, 1]))


def joined(blocks):
    return split_columns(stacked(*blocks))


def blocks_of(*refs):
    return [ref[s] for ref in refs for s in range(ref.shape[0])]


def own_slots(matrix, sides, groups):
    size = groups[0][0].shape[0]
    slots = len(groups[0])
    parts = []
    for s in range(slots):
        columns = [slice((side * slots + s) * size, (side * slots + s + 1) * size) for side in sides]
        high = [matrix[s * size:(s + 1) * size, c] for c in columns]
        low = [matrix[(slots + s) * size:(slots + s + 1) * size, c] for c in columns]
        left = stacked(jnp.concatenate(high, axis=1), jnp.concatenate(low, axis=1))
        parts.append(product(left, joined([group[s] for group in groups])))
    return stacked(*parts).reshape(slots, size, -1)


def near(matrix, field):
    columns = 2 * (matrix.shape[1] // 3)
    return product(matrix[:, :columns], field)


def far(matrix, field):
    columns = 2 * (matrix.shape[1] // 3)
    return product(matrix[:, columns:], field)


def level_blocks(down, mid):
    left = split_rows(jnp.concatenate([down[0], down[1]], axis=1))
    coarse = product(left, joined((mid[0], mid[1]))) + 0.5 * (mid[0] + mid[1])
    return [mid[0], coarse, mid[1]]


def rows_of(ref):
    size = ref.shape[-1]
    return [ref[k * size:(k + 1) * size, :] for k in range(2)]


def first_fine_kernel(matrix, own, *rest):
    *core, part = rest

    @pl.when(lax.axis_index("lvl") == 0)
    def _():
        part[...] = near(matrix, joined(blocks_of(own, *core))).reshape(part.shape)


def first_near_kernel(fine_part, matrix, own, down_own, down_core, mid_own, mid_core, mid_core_last, part, level):
    @pl.when(lax.axis_index("lvl") == 0)
    def _():
        level[...] = own[...]

    @pl.when(lax.axis_index("lvl") != 0)
    def _():
        here = level_blocks(down_own, blocks_of(mid_own))
        beside = level_blocks(down_core, blocks_of(mid_core, mid_core_last))
        level[...] = stacked(*here).reshape(level.shape)
        part[...] = own_slots(matrix, (0, 1), (here, beside))


def start_near_kernel(matrix, own, down_own, down_core, mid_own, mid_core, part, level):
    @pl.when(lax.axis_index("lvl") == 0)
    def _():
        level[...] = own[...]
        part[...] = near(matrix, joined(blocks_of(own, down_core))).reshape(part.shape)

    @pl.when(lax.axis_index("lvl") != 0)
    def _():
        here = level_blocks(down_own, blocks_of(mid_own))
        beside = level_blocks(down_core, blocks_of(mid_core))
        level[...] = stacked(*here).reshape(level.shape)
        part[...] = own_slots(matrix, (0, 1), (here, beside))


def start_far_kernel(matrix, part, cross, down_cross, skewed, first):
    @pl.when(lax.axis_index("lvl") == 0)
    def _():
        first[...] = part[...] + far(matrix, joined(blocks_of(cross))).reshape(first.shape)

    @pl.when(lax.axis_index("lvl") != 0)
    def _():
        beside = level_blocks(rows_of(down_cross), rows_of(skewed))
        first[...] = part[...] + own_slots(matrix, (2,), (beside,))


def first_far_kernel(matrix, part, cross, down_cross, skewed, first):
    @pl.when(lax.axis_index("lvl") == 0)
    def _():
        first[...] = part[...] + far(matrix, joined(blocks_of(cross))).reshape(first.shape)

    @pl.when(lax.axis_index("lvl") != 0)
    def _():
        beside = level_blocks(rows_of(down_cross), rows_of(skewed))
        first[...] = part[...] + own_slots(matrix, (2,), (beside,))


def near_kernel(matrix, own, core, core_last, *rest):
    part = rest[-1]

    @pl.when(lax.axis_index("lvl") == 0)
    def _():
        part[...] = near(matrix, joined(blocks_of(own, core, core_last))).reshape(part.shape)

    @pl.when(lax.axis_index("lvl") != 0)
    def _():
        part[...] = own_slots(matrix, (0, 1), (blocks_of(own), blocks_of(core, core_last)))


def fix_kernel(matrix, level, own, part, cross, prolong, smooth, fixes):
    @pl.when(lax.axis_index("lvl") == 0)
    def _():
        fixes[...] = jnp.zeros_like(fixes)

    @pl.when(lax.axis_index("lvl") != 0)
    def _():
        second = part[...] + own_slots(matrix, (2,), (blocks_of(cross),))
        value = COEF_ZERO * level[...] + COEF_ONE * own[...] + COEF_TWO * second
        coarse = value[1]
        size = coarse.shape[0]
        up = product(prolong[:4 * size, :size], split_columns(coarse))
        low, high = value[0] + up[:size], value[2] + up[size:]
        fixes[0] = low + coarse
        fixes[1] = high + coarse
        smooth[0] = low
        smooth[1] = coarse
        smooth[2] = high


def smooth_kernel(passed, matrix, level, own, part, cross, *rest):
    smooth = rest[-1]

    @pl.when(lax.axis_index("lvl") == 0)
    def _():
        second = part[...] + far(matrix, joined(blocks_of(cross))).reshape(part.shape)
        value = COEF_ZERO * level[...] + COEF_ONE * own[...] + COEF_TWO * second
        smooth[...] = value if len(rest) == 1 else rest[0][...] + value


def solution_kernel(smooth, fixes, prolong, result):
    @pl.when(lax.axis_index("lvl") == 0)
    def _():
        result[...] = smooth[...] + product(prolong[...], joined(blocks_of(fixes))).reshape(smooth.shape)

    @pl.when(lax.axis_index("lvl") != 0)
    def _():
        result[...] = smooth[...]


def tall_kernel(matrix, restrict, tall):
    big, wide = matrix.shape[0] // 2, restrict.shape[0] // 2

    @pl.when(lax.axis_index("lvl") == 0)
    def _():
        tall[:big, :] = matrix[:big, :]
        tall[big + wide:2 * big + wide, :] = matrix[big:, :]
        for c in range(0, matrix.shape[1], big):
            right = jnp.concatenate([matrix[:big, c:c + big], matrix[big:, c:c + big]], axis=1)
            high, low = split(product(restrict[...], right))
            tall[big:big + wide, c:c + big] = high
            tall[2 * big + wide:, c:c + big] = low


def residual_near_kernel(tall, own, core, core_last, part):
    @pl.when(lax.axis_index("lvl") == 0)
    def _():
        part[...] = near(tall, joined(blocks_of(own, core, core_last)))


def residual_mid_kernel(tall, part, cross, before, mids, skewed):
    size = mids.shape[1]
    big, half = part.shape[0] - 2 * size, tall.shape[0] // 2

    @pl.when(lax.axis_index("lvl") == 0)
    def _():
        columns = 2 * (tall.shape[1] // 3)
        left = stacked(tall[big:half, columns:], tall[half + big:, columns:])
        value = part[big:, :] + product(left, joined(blocks_of(cross)))
        store_mids(before[...].reshape(2 * size, -1) - value, mids, skewed)

    @pl.when(lax.axis_index("lvl") != 0)
    def _():
        mids[...] = jnp.zeros_like(mids)
        skewed[...] = jnp.zeros_like(skewed)


def residual_far_kernel(matrix, part, cross, rhs, resid):
    big = rhs.shape[0] * rhs.shape[1]

    @pl.when(lax.axis_index("lvl") == 0)
    def _():
        value = part[:big, :] + far(matrix, joined(blocks_of(cross)))
        resid[...] = rhs[...] - value.reshape(rhs.shape)

    @pl.when(lax.axis_index("lvl") != 0)
    def _():
        resid[...] = jnp.zeros_like(resid)


def call(kernel, outs, args, anywhere=0, scratch=(), aliases={}):
    args = [pltpu.with_memory_space_constraint(a, pltpu.HBM) for a in args[:anywhere]] + list(args[anywhere:])
    spaces = [pl.BlockSpec(memory_space=pltpu.HBM)] * anywhere
    spaces += [pl.BlockSpec(memory_space=pltpu.VMEM)] * (len(args) - anywhere)
    return pl.pallas_call(
        kernel,
        out_shape=[jax.ShapeDtypeStruct(shape, dtype) for shape, dtype in outs],
        in_specs=spaces,
        out_specs=[pl.BlockSpec(memory_space=pltpu.VMEM)] * len(outs),
        scratch_shapes=scratch,
        input_output_aliases=aliases,
        compiler_params=pltpu.CompilerParams(vmem_limit_bytes=24 * 1024 * 1024),
        cost_estimate=pl.CostEstimate(flops=0, bytes_accessed=0, transcendentals=0),
    )(*args)


def swaps(rows):
    across = [0] + [r + 1 if r % 2 else r - 1 for r in range(1, rows - 1)] + [rows - 1]
    core = [(l * rows + r, l * rows + (r ^ 1)) for l in range(2) for r in range(rows)]
    cross = [(l * rows + r, l * rows + across[r]) for l in range(2) for r in range(1, rows - 1)]
    cross += [(l * rows + r, (1 - l) * rows + r) for l in range(2) for r in (0, rows - 1)]
    fine = [(r, across[r]) for r in range(1, rows - 1)] + [(0, rows - 1), (rows - 1, 0)]
    fine += [(rows + r, rows + (r ^ 1)) for r in range(rows)]
    short = [(r, across[r]) for r in range(1, rows - 1)] + [(rows + r, rows + (r ^ 1)) for r in range(2, rows - 2)]
    for end, beside in ((0, 1), (rows - 1, rows - 2)):
        short += [(end, rows + beside), (rows + beside, rows + end), (rows + end, end)]
    other = [(r, r ^ 1) for r in range(2, rows - 2)] + [(rows + r, rows + across[r]) for r in range(1, rows - 1)]
    for end, beside in ((0, 1), (rows - 1, rows - 2)):
        other += [(rows + end, end), (end, beside), (beside, rows + end)]
    level = [(l * rows + r, (1 - l) * rows + r) for l in range(2) for r in range(rows)]
    skew = [(r, rows + across[r]) for r in range(1, rows - 1)]
    skew += [(rows + r, r) for r in range(rows) if r not in (1, rows - 2)]
    for end, beside in ((0, 1), (rows - 1, rows - 2)):
        skew += [(end, beside), (rows + beside, rows + end)]
    return tuple((lambda x, pairs=pairs: lax.ppermute(x, ("lvl", "row"), pairs)) for pairs in (core, cross, fine, short, other, level, skew))


def paired(rhs, op_tiles, op_cols, link_tiles, level_links):
    core, cross, fine, short, other, level, skew = swaps(lax.axis_size("row"))
    right, tiles, links = rhs[0, 0], op_tiles[0, 0], link_tiles[0, 0]
    slots, size, width = right.shape
    blocks, pair = (right.shape, F32), ((2, size, width), F32)
    big = slots * size
    codes, goals = jnp.swapaxes(op_cols, 1, 2), jnp.swapaxes(level_links, 2, 3)
    long = ((2 * size + 8, width), F32)
    mids, skewed, payload, wide, restrict = call(
        restrict_kernel,
        [pair, long, blocks, ((2 * size + 8, width), F32), ((4 * size, big), BF16)],
        [goals, right, links],
        anywhere=3,
        scratch=[
            pltpu.SMEM(goals.shape[2:], goals.dtype),
            pltpu.VMEM((slots, size, size), links.dtype),
            pltpu.SemaphoreType.DMA((3,)),
        ],
    )
    down = result = matrix = prolong = tall = None
    for cycle in range(CYCLES):
        if cycle > 0:
            result_cross = short(result)
            (part,) = call(
                residual_near_kernel,
                [((big + 2 * size, width), F32)],
                [tall, result, core(result[:-1]), core(result[-1:])],
            )
            mids, skewed = call(residual_mid_kernel, [pair, long], [tall, part, result_cross, mids])
            (payload,) = call(residual_far_kernel, [blocks], [matrix, part, result_cross, right])
        mid_here, mid_cross = level(mids), skew(skewed)
        if cycle == 0:
            beyond, beside, mid_core = short(payload), [core(payload)], [core(mid_here)]
            matrix, prolong = call(
                operator_kernel,
                [((2 * big, 3 * big), BF16), ((2 * big, 2 * size), BF16)],
                [codes, goals, links, tiles],
                anywhere=4,
                scratch=[
                    pltpu.SMEM(codes.shape[1:], codes.dtype),
                    pltpu.SMEM(goals.shape[2:], goals.dtype),
                    pltpu.VMEM(links.shape, links.dtype),
                    pltpu.VMEM(tiles.shape, tiles.dtype),
                    pltpu.VMEM((slots, 3 * slots, size, size), F32),
                    pltpu.SemaphoreType.DMA((3 + slots,)),
                ],
            )
            down = payload, beside[0], other(wide)
            part, level_resid = call(
                start_near_kernel,
                [blocks, blocks],
                [matrix, payload, *down[:2], mid_here, *mid_core],
            )
            (first,) = call(
                start_far_kernel,
                [blocks],
                [matrix, part, beyond, down[2], mid_cross],
            )
            (tall,) = call(tall_kernel, [((2 * big + 4 * size, 3 * big), BF16)], [matrix, restrict])
        else:
            beyond, beside = fine(payload), [core(payload)]
            mid_core = [core(mid_here[:1]), core(mid_here[1:])]
            (part,) = call(first_fine_kernel, [blocks], [matrix, payload, *beside])
            part, level_resid = call(
                first_near_kernel,
                [blocks, blocks],
                [part, matrix, payload, *down[:2], mid_here, *mid_core],
                aliases={0: 0},
            )
            (first,) = call(first_far_kernel, [blocks], [matrix, part, beyond, down[2], mid_cross])
        first_cross = cross(first)
        (part,) = call(near_kernel, [blocks], [matrix, first, core(first[:-1]), core(first[-1:])] + ([tall] if cycle == 0 else []))
        known = [matrix, level_resid, first, part, first_cross]
        smooth, fixes = call(fix_kernel, [blocks, pair], [*known, prolong])
        fixes = level(fixes)
        before = [] if cycle == 0 else [result]
        (smooth,) = call(smooth_kernel, [blocks], [smooth, *known, *before], aliases={0: 0})
        (result,) = call(solution_kernel, [blocks], [smooth, fixes, prolong])
    return result[None, None]


def body(rhs, *rest):
    rows = lax.axis_size("row")
    square = rhs.shape[-1] == rhs.shape[-2]
    plan = paired if lax.axis_size("lvl") == 2 and rows % 2 == 0 and rows > 2 and square else per_device
    return plan(rhs, *rest)


def solution(mesh):
    placed = (
        P("lvl", "row", None, None, None),
        P("lvl", "row", None, None, None, None),
        P("lvl", "row", None, None),
        P("lvl", "row", None, None, None, None),
        P("lvl", "row", None, None),
    )
    return jax.shard_map(
        body,
        mesh=mesh,
        in_specs=placed,
        out_specs=P("lvl", "row", None, None, None),
        check_vma=False,
    )
```
